128 devices in a mesh: row: 8 (over z_lo, x), col: 16 (over y, z_hi, core).
Axes of the slice: x: 4, y: 4, z: 4 (z_hi: 2, z_lo: 2; z = z_hi * 2 + z_lo), core: 2. Of those that a mesh axis runs over, the one named last changes fastest.
Arguments:
- a_tiles: bfloat16 [2176, 128, 128], P(('row', 'col')), may hold values from -0.375 to 0.375
- a_index: int32 [2176, 2], P(('row', 'col')), may hold values from 0 to 63, as said below
- b_tiles: bfloat16 [1280, 128, 128], P(('row', 'col')), may hold values from -6 to 6
- b_index: int32 [1280, 2], P(('row', 'col')), may hold values from 0 to 95, as said below
- row_dist: int32 [64], replicated, may hold values from 0 to 7, as said below
- col_dist: int32 [96], replicated, may hold values from 0 to 15, as said below
- c_index: int32 [3072, 2], P(('row', 'col')), may hold values from 0 to 95, as said below
Outputs:
- c_grid: bfloat16 [64, 96, 128, 128], P('row', 'col')
The draws below stay inside these ranges and needn't reach their ends.
Inputs may be any that keep to these rules, and one draw needn't show every extreme that they name: `a_index`: distinct tiles. Every tile stored on a device of grid row p has row_dist = p. Contraction block k belongs to image k mod 16; a tile's destination column is (image - p) mod 16. One device sends at most 2 tiles to any destination column; in every grid row one destination column receives exactly 2 from every device of the row, and every other destination column exactly one from every device. `b_index`: distinct tiles. Every tile stored on a device of grid column q has col_dist = q. A tile of image s has destination row (s - q) mod 8. One device sends at most 3 tiles to any destination row; in every grid column one destination row receives exactly 3 from every device of the column, and every other destination row exactly one from every device. `row_dist`: every grid row holds exactly 8 window block rows. `col_dist`: every grid column holds exactly 6 window block columns. `c_index`: each device holds 24 distinct pairs, all with row_dist equal to its grid row and col_dist equal to its grid column.
All inputs are finite; a program needn't handle non-finite values.
Results may differ from the reference program's by a relative error of at most 0.001.
Values may be sent and summed in bfloat16 or wider, within the bound.
No kernel may reach another device: no remote copies, remote signals or barrier semaphores. Data moves between devices by JAX's collectives and lax.ppermute only.
A program may use at most 128 MiB of HBM per device.

```python
import jax
import jax.numpy as jnp
from jax import lax

TILE = 128
RL = 8
CL = 6
KPI = 4
CAP_A = 2
CAP_B = 3
ATD = 17
BTD = 10
MR = 64
MC = 96
KW = 64
NA = 2176
NBT = 1280
CT = 24
N_ROW = 8
N_COL = 16


def shared_layout(key):
    row_perm = jax.random.permutation(jax.random.fold_in(key, 101), MR).astype(jnp.int32)
    col_perm = jax.random.permutation(jax.random.fold_in(key, 102), MC).astype(jnp.int32)
    return (row_perm, col_perm)


def grid_members(key):
    row_perm, col_perm = shared_layout(key)
    rows_of = jnp.argsort(row_perm).astype(jnp.int32).reshape(N_ROW, RL)
    cols_of = jnp.argsort(col_perm).astype(jnp.int32).reshape(N_COL, CL)
    return (rows_of, cols_of)


def many_perms(key, row_total, length):
    subkeys = jax.random.split(key, row_total)
    return jax.vmap(lambda subkey: jax.random.permutation(subkey, length))(subkeys).astype(jnp.int32)


def routed_targets(key, groups, members, targets, per_slot, capacity):
    forced = jax.random.randint(jax.random.fold_in(key, 1), (groups, 1, 1), 0, targets).astype(jnp.int32)
    others = many_perms(jax.random.fold_in(key, 2), groups * members, targets - 1)[:, :per_slot - capacity]
    others = others.reshape(groups, members, per_slot - capacity)
    unshuffled = jnp.concatenate([jnp.broadcast_to(forced, (groups, members, capacity)), (forced + 1 + others) % targets], axis=2)
    shuffle = many_perms(jax.random.fold_in(key, 3), groups * members, per_slot).reshape(groups, members, per_slot)
    return jnp.take_along_axis(unshuffled, shuffle, axis=2)


def landing_offsets(targets_of, targets):
    slot_count = targets_of.shape[2]
    positions = jnp.arange(slot_count)
    earlier = (targets_of[:, :, :, None] == targets_of[:, :, None, :]) & (positions[None, None, None, :] < positions[None, None, :, None])
    within = jnp.sum(earlier, axis=3).astype(jnp.int32)
    counts = jnp.sum(targets_of[:, :, :, None] == jnp.arange(targets)[None, None, None, :], axis=2).astype(jnp.int32)
    before = jnp.cumsum(counts, axis=1) - counts
    return jnp.take_along_axis(before, targets_of, axis=2) + within


def left_pattern(key):
    rows_of, cols_of = grid_members(key)
    local_key = jax.random.fold_in(key, 201)
    targets_of = routed_targets(local_key, N_ROW, N_COL, N_COL, ATD, CAP_A)
    offset = landing_offsets(targets_of, N_COL)
    places = many_perms(jax.random.fold_in(local_key, 4), N_ROW * N_COL, RL * KPI).reshape(N_ROW, N_COL, RL * KPI)
    grid_row = jnp.arange(N_ROW)[:, None, None]
    position = places[grid_row, targets_of, offset]
    image = (grid_row + targets_of) % N_COL
    block_row = rows_of[grid_row, position // KPI]
    block_k = position % KPI * N_COL + image
    pairs = jnp.stack([block_row, block_k], axis=3)
    return pairs.reshape(N_ROW * N_COL * ATD, 2).astype(jnp.int32)


def right_pattern(key):
    rows_of, cols_of = grid_members(key)
    local_key = jax.random.fold_in(key, 202)
    targets_of = routed_targets(local_key, N_COL, N_ROW, N_ROW, BTD, CAP_B)
    offset = landing_offsets(targets_of, N_ROW)
    places = many_perms(jax.random.fold_in(local_key, 4), N_COL * N_ROW, 2 * KPI * CL).reshape(N_COL, N_ROW, 2 * KPI * CL)
    grid_col = jnp.arange(N_COL)[:, None, None]
    position = places[grid_col, targets_of, offset]
    upper_half = position // (KPI * CL)
    remainder = position % (KPI * CL)
    image = (targets_of + grid_col + upper_half * N_ROW) % N_COL
    block_k = remainder // CL * N_COL + image
    block_col = cols_of[grid_col, remainder % CL]
    pairs = jnp.stack([block_k, block_col], axis=3)
    return jnp.transpose(pairs, (1, 0, 2, 3)).reshape(N_ROW * N_COL * BTD, 2).astype(jnp.int32)


def draw_a_index(key, part):
    pattern = left_pattern(key)
    return pattern


def draw_b_index(key, part):
    pattern = right_pattern(key)
    return pattern


def draw_row_dist(key, part):
    row_perm, col_perm = shared_layout(key)
    return (row_perm // RL).astype(jnp.int32)


def draw_col_dist(key, part):
    row_perm, col_perm = shared_layout(key)
    return (col_perm // CL).astype(jnp.int32)


def draw_c_index(key, part):
    rows_of, cols_of = grid_members(key)
    key = jax.random.fold_in(key, 15)
    chosen = many_perms(key, N_ROW * N_COL, RL * CL)[:, :CT].reshape(N_ROW, N_COL, CT)
    grid_row = jnp.arange(N_ROW)[:, None, None]
    grid_col = jnp.arange(N_COL)[None, :, None]
    block_row = rows_of[grid_row, chosen // CL]
    block_col = cols_of[grid_col, chosen % CL]
    pairs = jnp.stack([block_row, block_col], axis=3)
    return pairs.reshape(N_ROW * N_COL * CT, 2).astype(jnp.int32)


def shard_levels(stream_key, shape, shards, smallest, top_value):
    def one(dim, shards_of):
        steps = jax.random.uniform(jax.random.fold_in(jax.random.fold_in(stream_key, 6), dim), (shards_of,), jnp.float32, smallest / len(shards), top_value / len(shards))
        return jnp.repeat(jnp.exp(steps), shape[dim] // shards_of).reshape((-1,) + (1,) * (len(shape) - dim - 1))

    factor_of = one(*shards[0])
    for cut in shards[1:]:
        factor_of = factor_of * one(*cut)
    return factor_of


def bell_draw(stream_key, extent, scale, limit, cuts=(), kind=jnp.bfloat16):
    factor_of = shard_levels(stream_key, extent, cuts, -0.22, 0.18) if cuts else 1.0
    array = jax.random.normal(stream_key, extent, jnp.float32) * scale * factor_of
    return jnp.minimum(jnp.maximum(array, -limit), limit).astype(kind)


def setup_inputs(seed: int = 0) -> dict:
    key_of = jax.random.split(jax.random.key(seed), 8)
    return {
        "a_tiles": bell_draw(key_of[0], (NA, TILE, TILE), (2 * TILE) ** -0.5, 0.375, ((0, 128),)),
        "a_index": draw_a_index(jax.random.fold_in(key_of[7], 71), 0),
        "b_tiles": bell_draw(key_of[2], (NBT, TILE, TILE), 1.0, 6.0, ((0, 128),)),
        "b_index": draw_b_index(jax.random.fold_in(key_of[7], 71), 0),
        "row_dist": draw_row_dist(jax.random.fold_in(key_of[7], 71), 0),
        "col_dist": draw_col_dist(jax.random.fold_in(key_of[7], 71), 0),
        "c_index": draw_c_index(jax.random.fold_in(key_of[7], 71), 0),
    }


def reference(a_tiles, a_index, b_tiles, b_index, row_dist, col_dist, c_index):
    left_table = jnp.zeros((KW, MR, TILE, TILE), a_tiles.dtype).at[a_index[:, 1], a_index[:, 0]].set(a_tiles)
    left_table = left_table.reshape(KW, MR * TILE, TILE)

    def add_column(accumulated, scan_item):
        tile_value, location = scan_item
        column = jnp.dot(left_table[location[0]], tile_value, preferred_element_type=jnp.float32)
        return accumulated.at[location[1]].add(column), None

    start_value = jnp.zeros((MC, MR * TILE, TILE), jnp.float32)
    accumulated, _ = lax.scan(add_column, start_value, (b_tiles, b_index))
    blocks = accumulated.reshape(MC, MR, TILE, TILE)
    pattern_mask = jnp.zeros((MR, MC), jnp.float32).at[c_index[:, 0], c_index[:, 1]].set(1.0)
    row_order = jnp.argsort(row_dist, stable=True)
    col_order = jnp.argsort(col_dist, stable=True)
    picked = blocks[col_order][:, row_order]
    mask_picked = pattern_mask[row_order][:, col_order]
    result = jnp.transpose(picked, (1, 0, 2, 3)) * mask_picked[:, :, None, None]
    return result.astype(jnp.bfloat16)
```

```python
import functools

import jax
import jax.numpy as jnp
from jax import lax
from jax.experimental import pallas as pl
from jax.experimental.pallas import tpu as pltpu
from jax.sharding import PartitionSpec as P

TILE = 128
RL = 8
CL = 6
KW = 64
MR = 64
MC = 96
ATD = 17
BTD = 10
CT = 24
N_ROW = 8
N_COL = 16
LIST = 656

A_PLACES = [
    (y, z, c) for z in (0, 1) for y in (0, 3, 1, 2) for c in (0, 1)
]
B_PLACES = [(x, z) for z in (0, 1) for x in (0, 3, 1, 2)]


def col_move(x, dy=0, dz=0, dc=0, by_core=False):
    pairs = []
    for i in range(N_COL):
        y, z, c = i // 4, i // 2 % 2, i % 2
        step = -dy if by_core and c else dy
        pairs.append((i, (y + step) % 4 * 4 + (z + dz) % 2 * 2 + (c + dc) % 2))
    return lax.ppermute(x, "col", pairs)


def row_move(x, dx=0, dz=0):
    pairs = []
    for i in range(N_ROW):
        z, xx = i // 4, i % 4
        pairs.append((i, (z + dz) % 2 * 4 + (xx + dx) % 4))
    return lax.ppermute(x, "row", pairs)


def row_move_by_core(x):
    pairs = []
    for p in range(N_ROW):
        for q in range(N_COL):
            step = -1 if q % 2 else 1
            pairs.append((p * N_COL + q, (p // 4 * 4 + (p % 4 + step) % 4) * N_COL + q))
    return lax.ppermute(x, ("row", "col"), pairs)


def list_kernel(
    where_ref, aidx_ref, bidx_ref, rdist_ref, cdist_ref, cidx_ref,
    list_ref, start_ref, place_ref,
    row_place, col_place, slot_at, head, follow, b_col,
):
    p = where_ref[0]
    q = where_ref[1]

    def rank(n, dist_ref, mine, out):
        def body(r, count):
            hit = dist_ref[r] == mine
            out[r] = jnp.where(hit, count, 0)
            return count + hit.astype(jnp.int32)
        lax.fori_loop(0, n, body, jnp.int32(0))

    rank(MR, rdist_ref, p, row_place)
    rank(MC, cdist_ref, q, col_place)

    def clear(n, out):
        def body(r, _):
            out[r] = jnp.int32(-1)
            return 0
        lax.fori_loop(0, n, body, 0)

    clear(RL * CL, slot_at)
    clear(KW, head)

    def pattern(n, _):
        at = row_place[cidx_ref[2 * n]] * CL + col_place[cidx_ref[2 * n + 1]]
        slot_at[at] = n
        place_ref[n] = at
        return 0

    lax.fori_loop(0, CT, pattern, 0)

    for m, (sx, sz) in enumerate(B_PLACES):
        src = (p // 4 + sz) % 2 * 4 + (p % 4 + sx) % 4

        def link(t, _, src=src, m=m):
            at = (src * BTD + t) * 2
            k = bidx_ref[at]
            b = m * BTD + t
            b_col[b] = col_place[bidx_ref[at + 1]]
            follow[b] = head[k]
            head[k] = b
            return 0

        lax.fori_loop(0, BTD, link, 0)

    count = jnp.int32(0)
    for m, (sy, sz, sc) in enumerate(A_PLACES):
        src = (q // 4 + sy) % 4 * 4 + (q // 2 + sz) % 2 * 2 + (q + sc) % 2
        start_ref[m] = count

        def tile(t, count, src=src):
            at = (src * ATD + t) * 2
            i = row_place[aidx_ref[at]] * CL
            k = aidx_ref[at + 1]

            def more(state):
                return state[0] >= 0

            def step(state):
                b, count = state
                slot = slot_at[i + b_col[b]]
                list_ref[count] = t + b * 32 + slot * 4096
                return follow[b], count + (slot >= 0).astype(jnp.int32)

            return lax.while_loop(more, step, (head[k], count))[1]

        count = lax.fori_loop(0, ATD, tile, count)
    start_ref[len(A_PLACES)] = count


def build_lists(where, aidx, bidx, rdist, cdist, cidx):
    smem = pl.BlockSpec(memory_space=pltpu.SMEM)
    i32 = jnp.int32
    return pl.pallas_call(
        list_kernel,
        out_shape=(
            jax.ShapeDtypeStruct((LIST,), i32),
            jax.ShapeDtypeStruct((len(A_PLACES) + 1,), i32),
            jax.ShapeDtypeStruct((CT,), i32),
        ),
        in_specs=[smem] * 6,
        out_specs=(smem,) * 3,
        scratch_shapes=[
            pltpu.SMEM((MR,), i32),
            pltpu.SMEM((MC,), i32),
            pltpu.SMEM((RL * CL,), i32),
            pltpu.SMEM((KW,), i32),
            pltpu.SMEM((N_ROW * BTD,), i32),
            pltpu.SMEM((N_ROW * BTD,), i32),
        ],
    )(where, aidx, bidx, rdist, cdist, cidx)


def add_products(list_ref, start_ref, m, a_ref, b_ref, acc_ref):
    def body(n, _):
        entry = list_ref[n]
        t = entry & 31
        b = (entry >> 5) & 127
        slot = entry >> 12
        acc_ref[slot] += jnp.dot(a_ref[t], b_ref[b], preferred_element_type=jnp.float32)
        return 0

    lax.fori_loop(start_ref[m], start_ref[m + 1], body, 0)


def first_kernel(n_a, list_ref, start_ref, *refs):
    a_refs, b_refs = refs[:n_a], refs[n_a:n_a + len(B_PLACES)]
    acc_ref, b_ref = refs[n_a + len(B_PLACES):]
    acc_ref[...] = jnp.zeros_like(acc_ref)
    for m, ref in enumerate(b_refs):
        b_ref[m * BTD:(m + 1) * BTD] = ref[...]
    for m, ref in enumerate(a_refs):
        add_products(list_ref, start_ref, m, ref, b_ref, acc_ref)


def last_kernel(first, list_ref, start_ref, place_ref, acc_in, b_ref, *refs):
    a_refs, (out_ref, acc_ref) = refs[:-2], refs[-2:]
    out_ref[...] = jnp.zeros_like(out_ref)
    acc_ref[...] = acc_in[...]
    for m, ref in enumerate(a_refs):
        add_products(list_ref, start_ref, first + m, ref, b_ref, acc_ref)

    def body(n, _):
        out_ref[place_ref[n]] = acc_ref[n].astype(jnp.bfloat16)
        return 0

    lax.fori_loop(0, CT, body, 0)


def per_device(a_tiles, a_index, b_tiles, b_index, row_dist, col_dist, c_index):
    core = lax.axis_index("col") % 2
    where = jnp.stack([lax.axis_index("row"), lax.axis_index("col")]).astype(jnp.int32)
    aidx = lax.all_gather(a_index.reshape(2 * ATD), "col", tiled=True)
    bidx = lax.all_gather(b_index.reshape(2 * BTD), "row", tiled=True)
    entries, starts, places = build_lists(
        where, aidx, bidx, row_dist, col_dist, c_index.reshape(2 * CT)
    )

    a_blocks = []
    b_blocks = []
    a_far = col_move(a_tiles, dz=1)
    b_far = row_move(b_tiles, dz=1)
    for tiles in (a_tiles, a_far):
        up, down = col_move(tiles, dy=1), col_move(tiles, dy=-1)
        across = col_move(jnp.where(core == 0, up, down), dy=1, by_core=True)
        for block in (tiles, up, down, across):
            a_blocks += [block, col_move(block, dc=1)]
    for tiles in (b_tiles, b_far):
        up, down = row_move(tiles, dx=1), row_move(tiles, dx=-1)
        across = row_move_by_core(jnp.where(core == 0, up, down))
        b_blocks += [tiles, up, down, across]

    vmem = pl.BlockSpec(memory_space=pltpu.VMEM)
    smem = pl.BlockSpec(memory_space=pltpu.SMEM)
    early = len(A_PLACES) - 2
    acc, b_all = pl.pallas_call(
        functools.partial(first_kernel, early),
        out_shape=(
            jax.ShapeDtypeStruct((CT, TILE, TILE), jnp.float32),
            jax.ShapeDtypeStruct((N_ROW * BTD, TILE, TILE), jnp.bfloat16),
        ),
        in_specs=[smem] * 2 + [vmem] * (early + len(B_PLACES)),
        out_specs=(vmem,) * 2,
        compiler_params=pltpu.CompilerParams(vmem_limit_bytes=24 << 20),
        cost_estimate=pl.CostEstimate(flops=3_000_000_000, bytes_accessed=14_000_000, transcendentals=0),
    )(entries, starts, *a_blocks[:early], *b_blocks)
    out = pl.pallas_call(
        functools.partial(last_kernel, early),
        out_shape=jax.ShapeDtypeStruct((RL * CL, TILE, TILE), jnp.bfloat16),
        in_specs=[smem] * 3 + [vmem] * (2 + len(A_PLACES) - early),
        out_specs=vmem,
        scratch_shapes=[pltpu.VMEM((CT, TILE, TILE), jnp.float32)],
        compiler_params=pltpu.CompilerParams(vmem_limit_bytes=16 << 20),
        cost_estimate=pl.CostEstimate(flops=500_000_000, bytes_accessed=8_000_000, transcendentals=0),
    )(entries, starts, places, acc, b_all, *a_blocks[early:])
    return out.reshape(RL, CL, TILE, TILE)


def solution(mesh):
    in_specs = (
        P(("row", "col"), None, None),
        P(("row", "col"), None),
        P(("row", "col"), None, None),
        P(("row", "col"), None),
        P(),
        P(),
        P(("row", "col"), None),
    )
    out_specs = P("row", "col", None, None)
    return jax.shard_map(
        per_device, mesh=mesh, in_specs=in_specs, out_specs=out_specs, check_vma=False
    )
```

```python
import functools

import jax
import jax.numpy as jnp
from jax import lax
from jax.experimental import pallas as pl
from jax.experimental.pallas import tpu as pltpu
from jax.sharding import PartitionSpec as P

TILE = 128
RL = 8
CL = 6
KW = 64
MR = 64
MC = 96
ATD = 17
BTD = 10
CT = 24
N_ROW = 8
N_COL = 16
LABEL = 16
A_ROWS = ATD * TILE
B_ROWS = BTD * TILE
A_BLOCK = A_ROWS + LABEL
B_BLOCK = B_ROWS + LABEL
LIST = 640
GROUP = 4


def col_move(x, dy=0, dz=0, dc=0, by_core=False):
    pairs = []
    for i in range(N_COL):
        y, z, c = i // 4, i // 2 % 2, i % 2
        step = -dy if by_core and c else dy
        pairs.append((i, (y + step) % 4 * 4 + (z + dz) % 2 * 2 + (c + dc) % 2))
    return lax.ppermute(x, "col", pairs)


def row_move(x, dx=0, dz=0):
    pairs = []
    for i in range(N_ROW):
        z, xx = i // 4, i % 4
        pairs.append((i, (z + dz) % 2 * 4 + (xx + dx) % 4))
    return lax.ppermute(x, "row", pairs)


def row_move_by_core(x):
    pairs = []
    for p in range(N_ROW):
        for q in range(N_COL):
            step = -1 if q % 2 else 1
            pairs.append((p * N_COL + q, (p // 4 * 4 + (p % 4 + step) % 4) * N_COL + q))
    return lax.ppermute(x, ("row", "col"), pairs)


def with_labels(tiles, index):
    n = tiles.shape[0]
    labels = jnp.pad(index.T.astype(jnp.bfloat16), ((0, LABEL - 2), (0, TILE - n)))
    return jnp.concatenate([tiles.reshape(n * TILE, TILE), labels])


def copy_blocks(pieces, sems):
    copies = []
    for n, (src, dst) in enumerate(pieces):
        copy = pltpu.make_async_copy(src, dst, sems.at[n])
        copy.start()
        copies.append(copy)
    return copies


def read_labels(raw_ref):
    return raw_ref[:, :8, :].astype(jnp.float32)


def lanes_of(shape):
    return lax.broadcasted_iota(jnp.int32, shape, len(shape) - 1)


def rows_of(shape):
    return lax.broadcasted_iota(jnp.int32, shape, len(shape) - 2)


def small_dot(a, b, contract):
    return lax.dot_general(
        a.astype(jnp.bfloat16), b.astype(jnp.bfloat16), ((contract[:1], contract[1:]), ((), ())),
        preferred_element_type=jnp.float32,
    )


def make_list(n_blocks, labels, row_col, hot_k, slot_b, list_v):
    lane = lanes_of((8, TILE))
    sub = rows_of((8, TILE))
    one_up = jnp.where(lane < ATD, lane + 1, 0).astype(jnp.float32)
    k_rows = rows_of((KW, TILE)).astype(jnp.float32)
    held = jnp.zeros((16, KW), jnp.float32)
    for m in range(n_blocks):
        here = labels[m, 0:1, :] == row_col
        there = (labels[m, 1:2, :] == k_rows).astype(jnp.float32)
        tile = jnp.where(here, one_up, 0.0)
        block = jnp.where(here & (one_up > 0), float(m + 1), 0.0)
        held += small_dot(jnp.concatenate([tile, block]), there, (1, 1))
    found = small_dot(held, hot_k, (1, 0))
    tile, block = found[:8], found[8:]
    hit = (tile > 0) & (slot_b > 0)
    hits = hit.astype(jnp.float32)
    square = (TILE, TILE)
    before = (rows_of(square) < lanes_of(square)).astype(jnp.float32)
    place = small_dot(hits, before, (1, 0))
    in_row = small_dot(hits, jnp.ones(square, jnp.float32), (1, 0))
    for i in range(7):
        place += jnp.where(sub > i, in_row[i:i + 1], 0.0)
    place = jnp.where(hit, place, -1.0)
    total = jnp.sum(hits).astype(jnp.int32)
    b_tile = (lane - 6 * (lane >> 4)).astype(jnp.float32)
    fields = []
    for i in range(8):
        rows = (tile[i:i + 1] - 1, block[i:i + 1] - 1, b_tile[:1], CT + 1 - slot_b[i:i + 1])
        field = jnp.zeros((8, TILE), jnp.float32)
        for n, row in enumerate(rows):
            field = jnp.where(sub == n, row, field)
        fields.append(field)
    fields = jnp.concatenate(fields, axis=1).astype(jnp.bfloat16)

    for c in range(LIST // TILE):
        @pl.when(c * TILE < total)
        def _(c=c):
            spots = (rows_of(square) + c * TILE).astype(jnp.float32)
            chosen = jnp.concatenate(
                [(place[i:i + 1] == spots).astype(jnp.bfloat16) for i in range(8)], axis=1)
            got = small_dot(fields, chosen, (1, 1)).astype(jnp.int32)
            entry = got[0:1] + got[1:2] * ATD + got[2:3] * 512 + (CT - got[3:4]) * 65536
            list_v[c:c + 1, :] = entry
    return total


def store_list(list_v, list_ref, sem):
    copy = pltpu.make_async_copy(list_v, list_ref, sem)
    copy.start()
    copy.wait()


def add_products(total, list_ref, a_ref, b_ref, acc_ref):
    def body(g, _):
        found = []
        for u in range(GROUP):
            n = g * GROUP + u
            entry = list_ref[n >> 7, n & 127]
            a = pl.multiple_of((entry & 511) * TILE, TILE)
            b = pl.multiple_of(((entry >> 9) & 127) * TILE, TILE)
            product = jnp.dot(
                a_ref[pl.ds(a, TILE), :], b_ref[pl.ds(b, TILE), :],
                preferred_element_type=jnp.float32,
            )
            found.append((entry >> 16, product))
        for slot, product in found:
            acc_ref[slot] += product
        return 0

    lax.fori_loop(0, (total + GROUP - 1) // GROUP, body, 0)


def first_kernel(
    n_a, n_b, where_ref, rdist_ref, cdist_ref, cidx_ref, *refs,
):
    a_in, b_in = refs[:n_a], refs[n_a:n_a + n_b]
    (acc_ref, b_ref, row_col_ref, hot_k_ref, slot_b_ref, place_ref,
     a_ref, a_raw, b_raw, list_v, row_at, col_at, row_place, col_place, slot_ref, list_ref,
     a_sems, b_sems, raw_sems, list_sem) = refs[n_a + n_b:]
    raw = [(ref.at[pl.ds(A_ROWS, LABEL)], a_raw.at[m]) for m, ref in enumerate(a_in)]
    for m, ref in enumerate(b_in):
        for h in range(2):
            raw.append((ref.at[pl.ds(h * B_BLOCK + B_ROWS, LABEL)], b_raw.at[2 * m + h]))
    raw_copies = copy_blocks(raw, raw_sems)
    b_copies = copy_blocks(
        [(ref.at[pl.ds(h * B_BLOCK, B_ROWS)], b_ref.at[pl.ds((2 * m + h) * B_ROWS, B_ROWS)])
         for m, ref in enumerate(b_in) for h in range(2)], b_sems)
    a_copies = copy_blocks(
        [(ref.at[pl.ds(0, A_ROWS)], a_ref.at[pl.ds(m * A_ROWS, A_ROWS)])
         for m, ref in enumerate(a_in)], a_sems)
    acc_ref[...] = jnp.zeros_like(acc_ref)

    def rank(n, dist_ref, mine, at_ref, out):
        def body(r, count):
            out[r] = count
            at_ref[count] = r
            return count + jnp.where(dist_ref[r] == mine, 1, 0)
        lax.fori_loop(0, n, body, jnp.int32(0), unroll=8)

    rank(MR, rdist_ref, where_ref[0], row_at, row_place)
    rank(MC, cdist_ref, where_ref[1], col_at, col_place)

    def clear(n, _):
        slot_ref[n] = jnp.int32(0)
        return 0

    lax.fori_loop(0, RL * CL, clear, 0, unroll=8)

    def pattern(n, _):
        at = row_place[cidx_ref[n, 0]] * CL + col_place[cidx_ref[n, 1]]
        slot_ref[at] = n + 1
        place_ref[n] = at
        return 0

    lax.fori_loop(0, CT, pattern, 0, unroll=4)
    for copy in raw_copies:
        copy.wait()
    lane = lanes_of((8, TILE))
    sub = rows_of((8, TILE))
    b_labels = read_labels(b_raw)
    packed = jnp.zeros((8, TILE), jnp.float32)
    for m in range(2 * n_b):
        packed += pltpu.roll(jnp.where(lane < BTD, b_labels[m] + 1, 0.0), 16 * m, 1)
    hot_k_ref[...] = (packed[0:1] - 1 == rows_of((KW, TILE)).astype(jnp.float32)).astype(jnp.float32)
    row_col = jnp.zeros((8, TILE), jnp.float32)
    for i in range(RL):
        row_col = jnp.where(sub == i, row_at[i].astype(jnp.float32), row_col)
    row_col_ref[...] = row_col
    slot_b = jnp.zeros((8, TILE), jnp.float32)
    for j in range(CL):
        column = jnp.zeros((8, TILE), jnp.float32)
        for i in range(RL):
            column = jnp.where(sub == i, slot_ref[i * CL + j].astype(jnp.float32), column)
        slot_b = jnp.where(packed[1:2] - 1 == col_at[j].astype(jnp.float32), column, slot_b)
    slot_b_ref[...] = slot_b

    total = make_list(n_a, read_labels(a_raw), row_col, hot_k_ref[...], slot_b, list_v)
    store_list(list_v, list_ref, list_sem)
    for copy in b_copies + a_copies:
        copy.wait()
    add_products(total, list_ref, a_ref, b_ref, acc_ref)


def last_kernel(
    n_a, place_ref, acc_in, b_ref, row_col_ref, hot_k_ref, slot_b_ref, *refs,
):
    a_in = refs[:n_a]
    (out_ref, acc_ref, a_ref, a_raw, list_v, list_ref, a_sems, raw_sems, list_sem) = refs[n_a:]
    raw_copies = copy_blocks(
        [(ref.at[pl.ds(A_ROWS, LABEL)], a_raw.at[m]) for m, ref in enumerate(a_in)], raw_sems)
    a_copies = copy_blocks(
        [(ref.at[pl.ds(0, A_ROWS)], a_ref.at[pl.ds(m * A_ROWS, A_ROWS)])
         for m, ref in enumerate(a_in)], a_sems)
    for copy in raw_copies:
        copy.wait()
    total = make_list(
        n_a, read_labels(a_raw), row_col_ref[...], hot_k_ref[...], slot_b_ref[...], list_v)
    store_list(list_v, list_ref, list_sem)
    out_ref[...] = jnp.zeros_like(out_ref)
    acc_ref[...] = acc_in[...]
    for copy in a_copies:
        copy.wait()
    add_products(total, list_ref, a_ref, b_ref, acc_ref)

    def body(n, _):
        out_ref[place_ref[n]] = acc_ref[n].astype(jnp.bfloat16)
        return 0

    lax.fori_loop(0, CT, body, 0)


def per_device(a_tiles, a_index, b_tiles, b_index, row_dist, col_dist, c_index):
    core = lax.axis_index("col") % 2
    where = jnp.stack([lax.axis_index("row"), lax.axis_index("col")]).astype(jnp.int32)
    a_own = with_labels(a_tiles, a_index)
    b_own = with_labels(b_tiles, b_index)

    def by_core(first, second):
        return jnp.where(core == 0, first, second)

    def tie(x, *others):
        return lax.optimization_barrier((x, *others))[0]

    up0, down0 = col_move(a_own, dy=1), col_move(a_own, dy=-1)
    far = col_move(a_own, dz=1)
    b_near = jnp.concatenate([b_own, row_move(b_own, dz=1)])
    b_up, b_down = row_move(b_near, dx=1), row_move(b_near, dx=-1)
    pick0 = by_core(up0, down0)
    across0 = col_move(pick0, dy=1, by_core=True)
    far_sent = tie(far, pick0)
    up1, down1 = col_move(far_sent, dy=1), col_move(far_sent, dy=-1)
    b_across = row_move_by_core(by_core(b_up, b_down))
    pick1 = tie(by_core(up1, down1), across0)
    across1 = col_move(pick1, dy=1, by_core=True)

    early = [a_own, far, up0, down0, across0, up1, down1]
    early += [col_move(block, dc=1) for block in early]
    late = [across1, col_move(across1, dc=1)]
    b_blocks = [b_near, b_up, b_down, b_across]

    vmem = pl.BlockSpec(memory_space=pltpu.VMEM)
    smem = pl.BlockSpec(memory_space=pltpu.SMEM)
    anywhere = pl.BlockSpec(memory_space=pl.ANY)
    i32 = jnp.int32
    n_a, n_b = len(early), len(b_blocks)
    acc, b_all, row_col, hot_k, slot_b, places = pl.pallas_call(
        functools.partial(first_kernel, n_a, n_b),
        out_shape=(
            jax.ShapeDtypeStruct((CT + 1, TILE, TILE), jnp.float32),
            jax.ShapeDtypeStruct((2 * n_b * B_ROWS, TILE), jnp.bfloat16),
            jax.ShapeDtypeStruct((8, TILE), jnp.float32),
            jax.ShapeDtypeStruct((KW, TILE), jnp.float32),
            jax.ShapeDtypeStruct((8, TILE), jnp.float32),
            jax.ShapeDtypeStruct((CT,), i32),
        ),
        in_specs=[smem] * 4 + [anywhere] * (n_a + n_b),
        out_specs=(vmem,) * 5 + (smem,),
        scratch_shapes=[
            pltpu.VMEM((n_a * A_ROWS, TILE), jnp.bfloat16),
            pltpu.VMEM((n_a, LABEL, TILE), jnp.bfloat16),
            pltpu.VMEM((2 * n_b, LABEL, TILE), jnp.bfloat16),
            pltpu.VMEM((8, TILE), i32),
            pltpu.SMEM((MR,), i32),
            pltpu.SMEM((MC,), i32),
            pltpu.SMEM((MR,), i32),
            pltpu.SMEM((MC,), i32),
            pltpu.SMEM((RL * CL,), i32),
            pltpu.SMEM((8, TILE), i32),
            pltpu.SemaphoreType.DMA((n_a,)),
            pltpu.SemaphoreType.DMA((2 * n_b,)),
            pltpu.SemaphoreType.DMA((n_a + 2 * n_b,)),
            pltpu.SemaphoreType.DMA,
        ],
        compiler_params=pltpu.CompilerParams(vmem_limit_bytes=16 << 20),
        cost_estimate=pl.CostEstimate(flops=3_000_000_000, bytes_accessed=14_000_000, transcendentals=0),
    )(where, row_dist, col_dist, c_index, *early, *b_blocks)
    n_late = len(late)
    out = pl.pallas_call(
        functools.partial(last_kernel, n_late),
        out_shape=jax.ShapeDtypeStruct((RL * CL, TILE, TILE), jnp.bfloat16),
        in_specs=[smem] + [vmem] * 5 + [anywhere] * n_late,
        out_specs=vmem,
        scratch_shapes=[
            pltpu.VMEM((CT + 1, TILE, TILE), jnp.float32),
            pltpu.VMEM((n_late * A_ROWS, TILE), jnp.bfloat16),
            pltpu.VMEM((n_late, LABEL, TILE), jnp.bfloat16),
            pltpu.VMEM((8, TILE), i32),
            pltpu.SMEM((8, TILE), i32),
            pltpu.SemaphoreType.DMA((n_late,)),
            pltpu.SemaphoreType.DMA((n_late,)),
            pltpu.SemaphoreType.DMA,
        ],
        compiler_params=pltpu.CompilerParams(vmem_limit_bytes=12 << 20),
        cost_estimate=pl.CostEstimate(flops=500_000_000, bytes_accessed=8_000_000, transcendentals=0),
    )(places, acc, b_all, row_col, hot_k, slot_b, *late)
    return out.reshape(RL, CL, TILE, TILE)


def solution(mesh):
    in_specs = (
        P(("row", "col"), None, None),
        P(("row", "col"), None),
        P(("row", "col"), None, None),
        P(("row", "col"), None),
        P(),
        P(),
        P(("row", "col"), None),
    )
    out_specs = P("row", "col", None, None)
    return jax.shard_map(
        per_device, mesh=mesh, in_specs=in_specs, out_specs=out_specs, check_vma=False
    )
```

```python
import functools

import jax
import jax.numpy as jnp
from jax import lax
from jax.experimental import pallas as pl
from jax.experimental.pallas import tpu as pltpu
from jax.sharding import PartitionSpec as P

TILE = 128
RL = 8
CL = 6
KW = 64
MR = 64
MC = 96
ATD = 17
BTD = 10
CT = 24
N_ROW = 8
N_COL = 16
LABEL = 16
A_ROWS = ATD * TILE
B_ROWS = BTD * TILE
A_BLOCK = A_ROWS + LABEL
B_BLOCK = B_ROWS + LABEL
LIST = 640
GROUP = 8


def col_move(x, dy=0, dz=0, dc=0, by_core=False):
    pairs = []
    for i in range(N_COL):
        y, z, c = i // 4, i // 2 % 2, i % 2
        step = -dy if by_core and c else dy
        pairs.append((i, (y + step) % 4 * 4 + (z + dz) % 2 * 2 + (c + dc) % 2))
    return lax.ppermute(x, "col", pairs)


def row_move(x, dx=0, dz=0):
    pairs = []
    for i in range(N_ROW):
        z, xx = i // 4, i % 4
        pairs.append((i, (z + dz) % 2 * 4 + (xx + dx) % 4))
    return lax.ppermute(x, "row", pairs)


def row_move_by_core(x):
    pairs = []
    for p in range(N_ROW):
        for q in range(N_COL):
            step = -1 if q % 2 else 1
            pairs.append((p * N_COL + q, (p // 4 * 4 + (p % 4 + step) % 4) * N_COL + q))
    return lax.ppermute(x, ("row", "col"), pairs)


def with_labels(tiles, index):
    n = tiles.shape[0] * TILE
    inputs = [pltpu.with_memory_space_constraint(x, pltpu.HBM) for x in (tiles.reshape(n, TILE), index.T)]
    return pl.pallas_call(
        label_kernel,
        out_shape=jax.ShapeDtypeStruct((n + LABEL, TILE), jnp.bfloat16),
        in_specs=[pl.BlockSpec(memory_space=pl.ANY)] * 2,
        out_specs=pl.BlockSpec(memory_space=pltpu.VMEM),
        scratch_shapes=[
            pltpu.VMEM((2, tiles.shape[0]), jnp.int32),
            pltpu.VMEM((LABEL, TILE), jnp.float32),
            pltpu.SemaphoreType.DMA((2,)),
        ],
        compiler_params=pltpu.CompilerParams(vmem_limit_bytes=2 << 20),
    )(*inputs)


def copy_blocks(pieces, sems):
    copies = []
    for n, (src, dst) in enumerate(pieces):
        copy = pltpu.make_async_copy(src, dst, sems.at[n])
        copy.start()
        copies.append(copy)
    return copies


def read_labels(raw_ref):
    return raw_ref[:, :8, :].astype(jnp.float32)


def lanes_of(shape):
    return lax.broadcasted_iota(jnp.int32, shape, len(shape) - 1)


def rows_of(shape):
    return lax.broadcasted_iota(jnp.int32, shape, len(shape) - 2)


def small_dot(a, b, contract):
    return lax.dot_general(
        a.astype(jnp.bfloat16), b.astype(jnp.bfloat16), ((contract[:1], contract[1:]), ((), ())),
        preferred_element_type=jnp.float32,
    )


def make_list(n_blocks, labels, row_col, hot_k, slot_b, list_v):
    lane = lanes_of((8, TILE))
    sub = rows_of((8, TILE))
    one_up = jnp.where(lane < ATD, lane + 1, 0).astype(jnp.float32)
    k_rows = rows_of((KW, TILE)).astype(jnp.float32)
    held = jnp.zeros((16, KW), jnp.float32)
    for m in range(n_blocks):
        here = labels[m, 0:1, :] == row_col
        there = (labels[m, 1:2, :] == k_rows).astype(jnp.float32)
        tile = jnp.where(here, one_up, 0.0)
        block = jnp.where(here & (one_up > 0), float(m + 1), 0.0)
        held += small_dot(jnp.concatenate([tile, block]), there, (1, 1))
    found = small_dot(held, hot_k, (1, 0))
    tile, block = found[:8], found[8:]
    hit = (tile > 0) & (slot_b > 0)
    hits = hit.astype(jnp.float32)
    square = (TILE, TILE)
    before = (rows_of(square) < lanes_of(square)).astype(jnp.float32)
    place = small_dot(hits, before, (1, 0))
    in_row = small_dot(hits, jnp.ones(square, jnp.float32), (1, 0))
    for i in range(7):
        place += jnp.where(sub > i, in_row[i:i + 1], 0.0)
    place = jnp.where(hit, place, -1.0)
    total = jnp.sum(hits).astype(jnp.int32)
    b_tile = (lane - 6 * (lane >> 4)).astype(jnp.float32)
    fields = []
    for i in range(8):
        rows = (tile[i:i + 1] - 1, block[i:i + 1] - 1, b_tile[:1], CT + 1 - slot_b[i:i + 1])
        field = jnp.zeros((8, TILE), jnp.float32)
        for n, row in enumerate(rows):
            field = jnp.where(sub == n, row, field)
        fields.append(field)
    fields = jnp.concatenate(fields, axis=1).astype(jnp.bfloat16)

    for c in range(LIST // TILE):
        @pl.when(c * TILE < total)
        def _(c=c):
            spots = (rows_of(square) + c * TILE).astype(jnp.float32)
            chosen = jnp.concatenate(
                [(place[i:i + 1] == spots).astype(jnp.bfloat16) for i in range(8)], axis=1)
            got = small_dot(fields, chosen, (1, 1)).astype(jnp.int32)
            entry = got[0:1] + got[1:2] * ATD + got[2:3] * 512 + (CT - got[3:4]) * 65536
            list_v[c:c + 1, :] = entry
    return total


def store_list(list_v, list_ref, sem):
    copy = pltpu.make_async_copy(list_v, list_ref, sem)
    copy.start()
    copy.wait()


def add_products(total, list_ref, a_ref, b_ref, acc_ref):
    def body(g, _):
        found = []
        for u in range(GROUP):
            n = g * GROUP + u
            entry = list_ref[n >> 7, n & 127]
            a = pl.multiple_of((entry & 511) * TILE, TILE)
            b = pl.multiple_of(((entry >> 9) & 127) * TILE, TILE)
            product = jnp.dot(
                a_ref[pl.ds(a, TILE), :], b_ref[pl.ds(b, TILE), :],
                preferred_element_type=jnp.float32,
            )
            found.append((entry >> 16, product))
        for slot, product in found:
            acc_ref[slot] += product
        return 0

    lax.fori_loop(0, (total + GROUP - 1) // GROUP, body, 0)


def product_kernel(
    n_a, n_b, where_ref, rdist_ref, cdist_ref, cidx_ref, *refs,
):
    a_in, b_in = refs[:n_a], refs[n_a:n_a + n_b]
    (out_ref, acc_ref, a_ref, b_ref, a_raw, b_raw, list_v,
     row_at, col_at, row_place, col_place, slot_ref, place_ref, list_ref,
     a_sems, b_sems, raw_sems, list_sem) = refs[n_a + n_b:]
    raw_copies = copy_blocks(
        [(ref.at[pl.ds(A_ROWS, LABEL)], a_raw.at[m]) for m, ref in enumerate(a_in)]
        + [(ref.at[pl.ds(B_ROWS, LABEL)], b_raw.at[m]) for m, ref in enumerate(b_in)], raw_sems)
    b_copies = copy_blocks(
        [(ref.at[pl.ds(0, B_ROWS)], b_ref.at[pl.ds(m * B_ROWS, B_ROWS)])
         for m, ref in enumerate(b_in)], b_sems)
    a_copies = copy_blocks(
        [(ref.at[pl.ds(0, A_ROWS)], a_ref.at[pl.ds(m * A_ROWS, A_ROWS)])
         for m, ref in enumerate(a_in)], a_sems)

    def rank(n, dist_ref, mine, at_ref, out):
        def body(r, count):
            out[r] = count
            at_ref[count] = r
            return count + jnp.where(dist_ref[r] == mine, 1, 0)
        lax.fori_loop(0, n, body, jnp.int32(0), unroll=8)

    rank(MR, rdist_ref, where_ref[0], row_at, row_place)
    rank(MC, cdist_ref, where_ref[1], col_at, col_place)

    def clear(n, _):
        slot_ref[n] = jnp.int32(0)
        return 0

    lax.fori_loop(0, RL * CL, clear, 0, unroll=8)

    def pattern(n, _):
        at = row_place[cidx_ref[n, 0]] * CL + col_place[cidx_ref[n, 1]]
        slot_ref[at] = n + 1
        place_ref[n] = at
        return 0

    lax.fori_loop(0, CT, pattern, 0, unroll=4)
    acc_ref[...] = jnp.zeros_like(acc_ref)
    out_ref[...] = jnp.zeros_like(out_ref)
    for copy in raw_copies:
        copy.wait()
    lane = lanes_of((8, TILE))
    sub = rows_of((8, TILE))
    b_labels = read_labels(b_raw)
    packed = jnp.zeros((8, TILE), jnp.float32)
    for m in range(n_b):
        packed += pltpu.roll(jnp.where(lane < BTD, b_labels[m] + 1, 0.0), 16 * m, 1)
    hot_k = (packed[0:1] - 1 == rows_of((KW, TILE)).astype(jnp.float32)).astype(jnp.float32)
    row_col = jnp.zeros((8, TILE), jnp.float32)
    for i in range(RL):
        row_col = jnp.where(sub == i, row_at[i].astype(jnp.float32), row_col)
    slot_b = jnp.zeros((8, TILE), jnp.float32)
    for j in range(CL):
        column = jnp.zeros((8, TILE), jnp.float32)
        for i in range(RL):
            column = jnp.where(sub == i, slot_ref[i * CL + j].astype(jnp.float32), column)
        slot_b = jnp.where(packed[1:2] - 1 == col_at[j].astype(jnp.float32), column, slot_b)

    total = make_list(n_a, read_labels(a_raw), row_col, hot_k, slot_b, list_v)
    store_list(list_v, list_ref, list_sem)
    for copy in b_copies + a_copies:
        copy.wait()
    add_products(total, list_ref, a_ref, b_ref, acc_ref)

    def finish(n, _):
        out_ref[place_ref[n]] = acc_ref[n].astype(jnp.bfloat16)
        return 0

    lax.fori_loop(0, CT, finish, 0, unroll=4)


def label_kernel(tiles_ref, index_ref, out_ref, index_v, labels_ref, sems):
    n = tiles_ref.shape[0]
    tiles_copy = pltpu.make_async_copy(tiles_ref, out_ref.at[pl.ds(0, n)], sems.at[0])
    index_copy = pltpu.make_async_copy(index_ref, index_v, sems.at[1])
    index_copy.start()
    tiles_copy.start()
    labels_ref[...] = jnp.zeros_like(labels_ref)
    index_copy.wait()
    labels_ref[0:2, 0:n // TILE] = index_v[...].astype(jnp.float32)
    out_ref[n:n + LABEL] = labels_ref[...].astype(jnp.bfloat16)
    tiles_copy.wait()


def per_device(a_tiles, a_index, b_tiles, b_index, row_dist, col_dist, c_index):
    core = lax.axis_index("col") % 2
    where = jnp.stack([lax.axis_index("row"), lax.axis_index("col")]).astype(jnp.int32)
    tokens = []

    def by_core(first, second):
        return jnp.where(core == 0, first, second)

    def after(x, *others):
        tied = lax.optimization_barrier((x, *[other[:16] for other in others]))
        tokens.extend(tied[1:])
        return tied[0]

    a_own = with_labels(a_tiles, a_index)
    b_own = with_labels(b_tiles, b_index)
    up0, down0 = col_move(a_own, dy=1), col_move(a_own, dy=-1)
    far = col_move(a_own, dz=1)
    b_up0, b_down0 = row_move(b_own, dx=1), row_move(b_own, dx=-1)
    pick0 = by_core(up0, down0)
    across0 = col_move(pick0, dy=1, by_core=True)
    b_pick0 = by_core(b_up0, b_down0)
    b_across0 = row_move_by_core(after(b_pick0, pick0))
    b_far = row_move(b_own, dz=1)
    up1, down1 = col_move(after(far, pick0), dy=1), col_move(after(far, pick0), dy=-1)
    b_up1, b_down1 = row_move(b_far, dx=1), row_move(b_far, dx=-1)
    across1 = col_move(across0, dz=1)
    b_across1 = row_move_by_core(by_core(b_up1, b_down1))
    a_blocks = [a_own, up0, down0, across0, far, up1, down1, across1]
    sent = [a_own, up0, down0, across0, far, up1, down1, across1]
    a_blocks += [col_move(block, dc=1) for block in sent]
    b_blocks = [b_own, b_up0, b_down0, b_across0, b_far, b_up1, b_down1, b_across1]
    vmem = pl.BlockSpec(memory_space=pltpu.VMEM)
    smem = pl.BlockSpec(memory_space=pltpu.SMEM)
    anywhere = pl.BlockSpec(memory_space=pl.ANY)
    i32 = jnp.int32
    n_a, n_b, n_t = len(a_blocks), len(b_blocks), len(tokens)

    def kernel(*refs):
        inputs = 4 + n_a + n_b
        product_kernel(n_a, n_b, *refs[:inputs], *refs[inputs + n_t:])

    out = pl.pallas_call(
        kernel,
        out_shape=jax.ShapeDtypeStruct((RL * CL, TILE, TILE), jnp.bfloat16),
        in_specs=[smem] * 4 + [anywhere] * (n_a + n_b + n_t),
        out_specs=vmem,
        scratch_shapes=[
            pltpu.VMEM((CT + 1, TILE, TILE), jnp.float32),
            pltpu.VMEM((n_a * A_ROWS, TILE), jnp.bfloat16),
            pltpu.VMEM((n_b * B_ROWS, TILE), jnp.bfloat16),
            pltpu.VMEM((n_a, LABEL, TILE), jnp.bfloat16),
            pltpu.VMEM((n_b, LABEL, TILE), jnp.bfloat16),
            pltpu.VMEM((8, TILE), i32),
            pltpu.SMEM((MR,), i32),
            pltpu.SMEM((MC,), i32),
            pltpu.SMEM((MR,), i32),
            pltpu.SMEM((MC,), i32),
            pltpu.SMEM((RL * CL,), i32),
            pltpu.SMEM((CT,), i32),
            pltpu.SMEM((8, TILE), i32),
            pltpu.SemaphoreType.DMA((n_a,)),
            pltpu.SemaphoreType.DMA((n_b,)),
            pltpu.SemaphoreType.DMA((n_a + n_b,)),
            pltpu.SemaphoreType.DMA,
        ],
        compiler_params=pltpu.CompilerParams(vmem_limit_bytes=20 << 20),
        cost_estimate=pl.CostEstimate(flops=3_000_000_000, bytes_accessed=14_000_000, transcendentals=0),
    )(where, row_dist, col_dist, c_index, *[pltpu.with_memory_space_constraint(x, pltpu.HBM) for x in a_blocks + b_blocks], *tokens)
    return out.reshape(RL, CL, TILE, TILE)


def solution(mesh):
    in_specs = (
        P(("row", "col"), None, None),
        P(("row", "col"), None),
        P(("row", "col"), None, None),
        P(("row", "col"), None),
        P(),
        P(),
        P(("row", "col"), None),
    )
    out_specs = P("row", "col", None, None)
    return jax.shard_map(
        per_device, mesh=mesh, in_specs=in_specs, out_specs=out_specs, check_vma=False
    )
```

```python
import functools

import jax
import jax.numpy as jnp
from jax import lax
from jax.experimental import pallas as pl
from jax.experimental.pallas import tpu as pltpu
from jax.sharding import PartitionSpec as P

TILE = 128
RL = 8
CL = 6
KW = 64
MR = 64
MC = 96
ATD = 17
BTD = 10
CT = 24
N_ROW = 8
N_COL = 16
LABEL = 16
A_ROWS = ATD * TILE
B_ROWS = BTD * TILE
A_BLOCK = A_ROWS + LABEL
B_BLOCK = B_ROWS + LABEL
LIST = 640
GROUP = 32


def col_move(x, dy=0, dz=0, dc=0, by_core=False):
    pairs = []
    for i in range(N_COL):
        y, z, c = i // 4, i // 2 % 2, i % 2
        step = -dy if by_core and c else dy
        pairs.append((i, (y + step) % 4 * 4 + (z + dz) % 2 * 2 + (c + dc) % 2))
    return lax.ppermute(x, "col", pairs)


def row_move(x, dx=0, dz=0):
    pairs = []
    for i in range(N_ROW):
        z, xx = i // 4, i % 4
        pairs.append((i, (z + dz) % 2 * 4 + (xx + dx) % 4))
    return lax.ppermute(x, "row", pairs)


def row_move_by_core(x):
    pairs = []
    for p in range(N_ROW):
        for q in range(N_COL):
            step = -1 if q % 2 else 1
            pairs.append((p * N_COL + q, (p // 4 * 4 + (p % 4 + step) % 4) * N_COL + q))
    return lax.ppermute(x, ("row", "col"), pairs)


def with_labels(tiles, index):
    n = tiles.shape[0] * TILE
    inputs = [pltpu.with_memory_space_constraint(x, pltpu.HBM) for x in (tiles.reshape(n, TILE), index.T)]
    return pl.pallas_call(
        label_kernel,
        out_shape=jax.ShapeDtypeStruct((n + LABEL, TILE), jnp.bfloat16),
        in_specs=[pl.BlockSpec(memory_space=pl.ANY)] * 2,
        out_specs=pl.BlockSpec(memory_space=pltpu.VMEM),
        scratch_shapes=[
            pltpu.VMEM((2, tiles.shape[0]), jnp.int32),
            pltpu.VMEM((LABEL, TILE), jnp.float32),
            pltpu.SemaphoreType.DMA((2,)),
        ],
        compiler_params=pltpu.CompilerParams(vmem_limit_bytes=2 << 20),
    )(*inputs)


def copy_blocks(pieces, sems):
    copies = []
    for n, (src, dst) in enumerate(pieces):
        copy = pltpu.make_async_copy(src, dst, sems.at[n])
        copy.start()
        copies.append(copy)
    return copies


def read_labels(raw_ref):
    return raw_ref[:, :8, :].astype(jnp.float32)


def lanes_of(shape):
    return lax.broadcasted_iota(jnp.int32, shape, len(shape) - 1)


def rows_of(shape):
    return lax.broadcasted_iota(jnp.int32, shape, len(shape) - 2)


def small_dot(a, b, contract):
    return lax.dot_general(
        a.astype(jnp.bfloat16), b.astype(jnp.bfloat16), ((contract[:1], contract[1:]), ((), ())),
        preferred_element_type=jnp.float32,
    )


def make_list(n_blocks, labels, row_col, hot_k, slot_b, list_v):
    lane = lanes_of((8, TILE))
    sub = rows_of((8, TILE))
    one_up = jnp.where(lane < ATD, lane + 1, 0).astype(jnp.float32)
    k_rows = rows_of((KW, TILE)).astype(jnp.float32)
    held = jnp.zeros((16, KW), jnp.float32)
    for m in range(n_blocks):
        here = labels[m, 0:1, :] == row_col
        there = (labels[m, 1:2, :] == k_rows).astype(jnp.float32)
        tile = jnp.where(here, one_up, 0.0)
        block = jnp.where(here & (one_up > 0), float(m + 1), 0.0)
        held += small_dot(jnp.concatenate([tile, block]), there, (1, 1))
    found = small_dot(held, hot_k, (1, 0))
    tile, block = found[:8], found[8:]
    hit = (tile > 0) & (slot_b > 0)
    hits = hit.astype(jnp.float32)
    square = (TILE, TILE)
    before = (rows_of(square) < lanes_of(square)).astype(jnp.float32)
    place = small_dot(hits, before, (1, 0))
    in_row = small_dot(hits, jnp.ones(square, jnp.float32), (1, 0))
    for i in range(7):
        place += jnp.where(sub > i, in_row[i:i + 1], 0.0)
    place = jnp.where(hit, place, -1.0)
    total = jnp.sum(hits).astype(jnp.int32)
    b_tile = (lane - 6 * (lane >> 4)).astype(jnp.float32)
    fields = []
    for i in range(8):
        rows = (tile[i:i + 1] - 1, block[i:i + 1] - 1, b_tile[:1], CT + 1 - slot_b[i:i + 1])
        field = jnp.zeros((8, TILE), jnp.float32)
        for n, row in enumerate(rows):
            field = jnp.where(sub == n, row, field)
        fields.append(field)
    fields = jnp.concatenate(fields, axis=1).astype(jnp.bfloat16)

    for c in range(LIST // TILE):
        @pl.when(c * TILE < total)
        def _(c=c):
            spots = (rows_of(square) + c * TILE).astype(jnp.float32)
            chosen = jnp.concatenate(
                [(place[i:i + 1] == spots).astype(jnp.bfloat16) for i in range(8)], axis=1)
            got = small_dot(fields, chosen, (1, 1)).astype(jnp.int32)
            entry = got[0:1] + got[1:2] * ATD + got[2:3] * 512 + (CT - got[3:4]) * 65536
            list_v[c:c + 1, :] = entry
    return total


def store_list(list_v, list_ref, sem):
    copy = pltpu.make_async_copy(list_v, list_ref, sem)
    copy.start()
    copy.wait()


def add_products(total, list_ref, a_ref, b_ref, acc_ref):
    def body(g, _):
        found = []
        for u in range(GROUP):
            n = g * GROUP + u
            entry = list_ref[n >> 7, n & 127]
            a = pl.multiple_of((entry & 511) * TILE, TILE)
            b = pl.multiple_of(((entry >> 9) & 127) * TILE, TILE)
            product = jnp.dot(
                a_ref[pl.ds(a, TILE), :], b_ref[pl.ds(b, TILE), :],
                preferred_element_type=jnp.float32,
            )
            found.append((entry >> 16, product))
        for slot, product in found:
            acc_ref[slot] += product
        return 0

    lax.fori_loop(0, (total + GROUP - 1) // GROUP, body, 0)


def product_kernel(
    n_a, n_b, where_ref, rdist_ref, cdist_ref, cidx_ref, *refs,
):
    a_in, b_in = refs[:n_a], refs[n_a:n_a + n_b]
    (out_ref, acc_ref, a_ref, b_ref, a_raw, b_raw, list_v,
     row_at, col_at, row_place, col_place, slot_ref, place_ref, list_ref,
     a_sems, b_sems, raw_sems, list_sem) = refs[n_a + n_b:]
    raw_copies = copy_blocks(
        [(ref.at[pl.ds(A_ROWS, LABEL)], a_raw.at[m]) for m, ref in enumerate(a_in)]
        + [(ref.at[pl.ds(B_ROWS, LABEL)], b_raw.at[m]) for m, ref in enumerate(b_in)], raw_sems)
    b_copies = copy_blocks(
        [(ref.at[pl.ds(0, B_ROWS)], b_ref.at[pl.ds(m * B_ROWS, B_ROWS)])
         for m, ref in enumerate(b_in)], b_sems)
    a_copies = copy_blocks(
        [(ref.at[pl.ds(0, A_ROWS)], a_ref.at[pl.ds(m * A_ROWS, A_ROWS)])
         for m, ref in enumerate(a_in)], a_sems)

    def rank(n, dist_ref, mine, at_ref, out):
        def body(r, count):
            out[r] = count
            at_ref[count] = r
            return count + jnp.where(dist_ref[r] == mine, 1, 0)
        lax.fori_loop(0, n, body, jnp.int32(0), unroll=8)

    rank(MR, rdist_ref, where_ref[0], row_at, row_place)
    rank(MC, cdist_ref, where_ref[1], col_at, col_place)

    def clear(n, _):
        slot_ref[n] = jnp.int32(0)
        return 0

    lax.fori_loop(0, RL * CL, clear, 0, unroll=8)

    def pattern(n, _):
        at = row_place[cidx_ref[n, 0]] * CL + col_place[cidx_ref[n, 1]]
        slot_ref[at] = n + 1
        place_ref[n] = at
        return 0

    lax.fori_loop(0, CT, pattern, 0, unroll=4)
    acc_ref[...] = jnp.zeros_like(acc_ref)
    out_ref[...] = jnp.zeros_like(out_ref)
    for copy in raw_copies:
        copy.wait()
    lane = lanes_of((8, TILE))
    sub = rows_of((8, TILE))
    b_labels = read_labels(b_raw)
    packed = jnp.zeros((8, TILE), jnp.float32)
    for m in range(n_b):
        packed += pltpu.roll(jnp.where(lane < BTD, b_labels[m] + 1, 0.0), 16 * m, 1)
    hot_k = (packed[0:1] - 1 == rows_of((KW, TILE)).astype(jnp.float32)).astype(jnp.float32)
    row_col = jnp.zeros((8, TILE), jnp.float32)
    for i in range(RL):
        row_col = jnp.where(sub == i, row_at[i].astype(jnp.float32), row_col)
    slot_b = jnp.zeros((8, TILE), jnp.float32)
    for j in range(CL):
        column = jnp.zeros((8, TILE), jnp.float32)
        for i in range(RL):
            column = jnp.where(sub == i, slot_ref[i * CL + j].astype(jnp.float32), column)
        slot_b = jnp.where(packed[1:2] - 1 == col_at[j].astype(jnp.float32), column, slot_b)

    total = make_list(n_a, read_labels(a_raw), row_col, hot_k, slot_b, list_v)
    store_list(list_v, list_ref, list_sem)
    for copy in b_copies + a_copies:
        copy.wait()
    add_products(total, list_ref, a_ref, b_ref, acc_ref)

    def finish(n, _):
        out_ref[place_ref[n]] = acc_ref[n].astype(jnp.bfloat16)
        return 0

    lax.fori_loop(0, CT, finish, 0, unroll=4)


def label_kernel(tiles_ref, index_ref, out_ref, index_v, labels_ref, sems):
    n = tiles_ref.shape[0]
    tiles_copy = pltpu.make_async_copy(tiles_ref, out_ref.at[pl.ds(0, n)], sems.at[0])
    index_copy = pltpu.make_async_copy(index_ref, index_v, sems.at[1])
    index_copy.start()
    tiles_copy.start()
    labels_ref[...] = jnp.zeros_like(labels_ref)
    index_copy.wait()
    labels_ref[0:2, 0:n // TILE] = index_v[...].astype(jnp.float32)
    out_ref[n:n + LABEL] = labels_ref[...].astype(jnp.bfloat16)
    tiles_copy.wait()


def per_device(a_tiles, a_index, b_tiles, b_index, row_dist, col_dist, c_index):
    core = lax.axis_index("col") % 2
    where = jnp.stack([lax.axis_index("row"), lax.axis_index("col")]).astype(jnp.int32)
    tokens = []

    def by_core(first, second):
        return jnp.where(core == 0, first, second)

    def after(x, *others):
        tied = lax.optimization_barrier((x, *[other[:16] for other in others]))
        tokens.extend(tied[1:])
        return tied[0]

    a_own = with_labels(a_tiles, a_index)
    b_own = with_labels(b_tiles, b_index)
    up0, down0 = col_move(a_own, dy=1), col_move(a_own, dy=-1)
    far = col_move(a_own, dz=1)
    b_up0, b_down0 = row_move(b_own, dx=1), row_move(b_own, dx=-1)
    pick0 = by_core(up0, down0)
    across0 = col_move(pick0, dy=1, by_core=True)
    b_pick0 = by_core(b_up0, b_down0)
    b_across0 = row_move_by_core(after(b_pick0, pick0))
    b_far = row_move(b_own, dz=1)
    far_sent = after(far, pick0)
    up1, down1 = col_move(far_sent, dy=1), col_move(far_sent, dy=-1)
    b_up1, b_down1 = row_move(b_far, dx=1), row_move(b_far, dx=-1)
    across1 = col_move(across0, dz=1)
    b_across1 = row_move_by_core(by_core(b_up1, b_down1))
    a_blocks = [a_own, up0, down0, across0, far, up1, down1, across1]
    a_blocks += [col_move(block, dc=1) for block in a_blocks]
    b_blocks = [b_own, b_up0, b_down0, b_across0, b_far, b_up1, b_down1, b_across1]
    vmem = pl.BlockSpec(memory_space=pltpu.VMEM)
    smem = pl.BlockSpec(memory_space=pltpu.SMEM)
    anywhere = pl.BlockSpec(memory_space=pl.ANY)
    i32 = jnp.int32
    n_a, n_b, n_t = len(a_blocks), len(b_blocks), len(tokens)

    def kernel(*refs):
        inputs = 4 + n_a + n_b
        product_kernel(n_a, n_b, *refs[:inputs], *refs[inputs + n_t:])

    out = pl.pallas_call(
        kernel,
        out_shape=jax.ShapeDtypeStruct((RL * CL, TILE, TILE), jnp.bfloat16),
        in_specs=[smem] * 4 + [anywhere] * (n_a + n_b + n_t),
        out_specs=vmem,
        scratch_shapes=[
            pltpu.VMEM((CT + 1, TILE, TILE), jnp.float32),
            pltpu.VMEM((n_a * A_ROWS, TILE), jnp.bfloat16),
            pltpu.VMEM((n_b * B_ROWS, TILE), jnp.bfloat16),
            pltpu.VMEM((n_a, LABEL, TILE), jnp.bfloat16),
            pltpu.VMEM((n_b, LABEL, TILE), jnp.bfloat16),
            pltpu.VMEM((8, TILE), i32),
            pltpu.SMEM((MR,), i32),
            pltpu.SMEM((MC,), i32),
            pltpu.SMEM((MR,), i32),
            pltpu.SMEM((MC,), i32),
            pltpu.SMEM((RL * CL,), i32),
            pltpu.SMEM((CT,), i32),
            pltpu.SMEM((8, TILE), i32),
            pltpu.SemaphoreType.DMA((n_a,)),
            pltpu.SemaphoreType.DMA((n_b,)),
            pltpu.SemaphoreType.DMA((n_a + n_b,)),
            pltpu.SemaphoreType.DMA,
        ],
        compiler_params=pltpu.CompilerParams(vmem_limit_bytes=20 << 20),
        cost_estimate=pl.CostEstimate(flops=3_000_000_000, bytes_accessed=14_000_000, transcendentals=0),
    )(where, row_dist, col_dist, c_index, *[pltpu.with_memory_space_constraint(x, pltpu.HBM) for x in a_blocks + b_blocks], *tokens)
    return out.reshape(RL, CL, TILE, TILE)


def solution(mesh):
    in_specs = (
        P(("row", "col"), None, None),
        P(("row", "col"), None),
        P(("row", "col"), None, None),
        P(("row", "col"), None),
        P(),
        P(),
        P(("row", "col"), None),
    )
    out_specs = P("row", "col", None, None)
    return jax.shard_map(
        per_device, mesh=mesh, in_specs=in_specs, out_specs=out_specs, check_vma=False
    )
```

```python
import functools

import jax
import jax.numpy as jnp
from jax import lax
from jax.experimental import pallas as pl
from jax.experimental.pallas import tpu as pltpu
from jax.sharding import PartitionSpec as P

TILE = 128
RL = 8
CL = 6
KW = 64
MR = 64
MC = 96
ATD = 17
BTD = 10
CT = 24
N_ROW = 8
N_COL = 16
LABEL = 16
A_ROWS = ATD * TILE
B_ROWS = BTD * TILE
A_BLOCK = A_ROWS + LABEL
B_BLOCK = B_ROWS + LABEL
LIST = 640
LAST = (5, 6, 7, 13, 14, 15)
GROUP = 32


def col_move(x, dy=0, dz=0, dc=0, by_core=False):
    pairs = []
    for i in range(N_COL):
        y, z, c = i // 4, i // 2 % 2, i % 2
        step = -dy if by_core and c else dy
        pairs.append((i, (y + step) % 4 * 4 + (z + dz) % 2 * 2 + (c + dc) % 2))
    return lax.ppermute(x, "col", pairs)


def row_move(x, dx=0, dz=0):
    pairs = []
    for i in range(N_ROW):
        z, xx = i // 4, i % 4
        pairs.append((i, (z + dz) % 2 * 4 + (xx + dx) % 4))
    return lax.ppermute(x, "row", pairs)


def row_move_by_core(x):
    pairs = []
    for p in range(N_ROW):
        for q in range(N_COL):
            step = -1 if q % 2 else 1
            pairs.append((p * N_COL + q, (p // 4 * 4 + (p % 4 + step) % 4) * N_COL + q))
    return lax.ppermute(x, ("row", "col"), pairs)


def with_labels(a_tiles, a_index, b_tiles, b_index):
    inputs, shapes, scratch = [], [], []
    for tiles, index in ((a_tiles, a_index), (b_tiles, b_index)):
        n = tiles.shape[0] * TILE
        inputs += [tiles.reshape(n, TILE), index.T]
        shapes.append(jax.ShapeDtypeStruct((n + LABEL, TILE), jnp.bfloat16))
        scratch += [
            pltpu.VMEM((2, tiles.shape[0]), jnp.int32),
            pltpu.VMEM((LABEL, TILE), jnp.float32),
            pltpu.SemaphoreType.DMA((2,)),
        ]
    return pl.pallas_call(
        label_kernel,
        out_shape=tuple(shapes),
        in_specs=[pl.BlockSpec(memory_space=pl.ANY)] * 4,
        out_specs=(pl.BlockSpec(memory_space=pltpu.VMEM),) * 2,
        scratch_shapes=scratch,
        compiler_params=pltpu.CompilerParams(vmem_limit_bytes=3 << 20),
    )(*[pltpu.with_memory_space_constraint(x, pltpu.HBM) for x in inputs])


def copy_blocks(pieces, sems):
    copies = []
    for n, (src, dst) in enumerate(pieces):
        copy = pltpu.make_async_copy(src, dst, sems.at[n])
        copy.start()
        copies.append(copy)
    return copies


def read_labels(raw_ref):
    return raw_ref[:, :8, :].astype(jnp.float32)


def lanes_of(shape):
    return lax.broadcasted_iota(jnp.int32, shape, len(shape) - 1)


def rows_of(shape):
    return lax.broadcasted_iota(jnp.int32, shape, len(shape) - 2)


def small_dot(a, b, contract):
    return lax.dot_general(
        a.astype(jnp.bfloat16), b.astype(jnp.bfloat16), ((contract[:1], contract[1:]), ((), ())),
        preferred_element_type=jnp.float32,
    )


def make_list(n_blocks, labels, row_col, hot_k, slot_b, list_v):
    lane = lanes_of((8, TILE))
    sub = rows_of((8, TILE))
    one_up = jnp.where(lane < ATD, lane + 1, 0).astype(jnp.float32)
    k_rows = rows_of((KW, TILE)).astype(jnp.float32)
    held = jnp.zeros((16, KW), jnp.float32)
    for m in range(n_blocks):
        here = labels[m, 0:1, :] == row_col
        there = (labels[m, 1:2, :] == k_rows).astype(jnp.float32)
        tile = jnp.where(here, one_up, 0.0)
        block = jnp.where(here & (one_up > 0), float(m + 1), 0.0)
        held += small_dot(jnp.concatenate([tile, block]), there, (1, 1))
    found = small_dot(held, hot_k, (1, 0))
    tile, block = found[:8], found[8:]
    hit = (tile > 0) & (slot_b > 0)
    hits = hit.astype(jnp.float32)
    square = (TILE, TILE)
    before = (rows_of(square) < lanes_of(square)).astype(jnp.float32)
    place = small_dot(hits, before, (1, 0))
    in_row = small_dot(hits, jnp.ones(square, jnp.float32), (1, 0))
    for i in range(7):
        place += jnp.where(sub > i, in_row[i:i + 1], 0.0)
    place = jnp.where(hit, place, -1.0)
    total = jnp.sum(hits).astype(jnp.int32)
    b_tile = (lane - 6 * (lane >> 4)).astype(jnp.float32)
    fields = []
    for i in range(8):
        rows = (tile[i:i + 1] - 1, block[i:i + 1] - 1, b_tile[:1], CT + 1 - slot_b[i:i + 1])
        field = jnp.zeros((8, TILE), jnp.float32)
        for n, row in enumerate(rows):
            field = jnp.where(sub == n, row, field)
        fields.append(field)
    fields = jnp.concatenate(fields, axis=1).astype(jnp.bfloat16)

    for c in range(LIST // TILE):
        @pl.when(c * TILE < total)
        def _(c=c):
            spots = (rows_of(square) + c * TILE).astype(jnp.float32)
            chosen = jnp.concatenate(
                [(place[i:i + 1] == spots).astype(jnp.bfloat16) for i in range(8)], axis=1)
            got = small_dot(fields, chosen, (1, 1)).astype(jnp.int32)
            entry = got[0:1] + got[1:2] * ATD + got[2:3] * 512 + (CT - got[3:4]) * 65536
            list_v[c:c + 1, :] = entry
    return total


def store_list(list_v, list_ref, sem):
    copy = pltpu.make_async_copy(list_v, list_ref, sem)
    copy.start()
    copy.wait()


def add_products(total, list_ref, a_ref, b_ref, acc_ref):
    def body(g, _):
        found = []
        for u in range(GROUP):
            n = g * GROUP + u
            entry = list_ref[n >> 7, n & 127]
            a = pl.multiple_of((entry & 511) * TILE, TILE)
            b = pl.multiple_of(((entry >> 9) & 127) * TILE, TILE)
            product = jnp.dot(
                a_ref[pl.ds(a, TILE), :], b_ref[pl.ds(b, TILE), :],
                preferred_element_type=jnp.float32,
            )
            found.append((entry >> 16, product))
        for slot, product in found:
            acc_ref[slot] += product
        return 0

    lax.fori_loop(0, (total + GROUP - 1) // GROUP, body, 0)


def product_kernel(
    n_a, n_b, where_ref, rdist_ref, cdist_ref, cidx_ref, *refs,
):
    a_in, b_in = refs[:n_a], refs[n_a:n_a + n_b]
    (out_ref, acc_ref, a_ref, b_ref, a_raw, b_raw, list_v,
     row_at, col_at, row_place, col_place, slot_ref, place_ref, list_ref,
     a_sems, b_sems, raw_sems, list_sem) = refs[n_a + n_b:]
    raw_copies = copy_blocks(
        [(ref.at[pl.ds(A_ROWS, LABEL)], a_raw.at[m]) for m, ref in enumerate(a_in)]
        + [(ref.at[pl.ds(B_ROWS, LABEL)], b_raw.at[m]) for m, ref in enumerate(b_in)], raw_sems)
    b_copies = copy_blocks(
        [(ref.at[pl.ds(0, B_ROWS)], b_ref.at[pl.ds(m * B_ROWS, B_ROWS)])
         for m, ref in enumerate(b_in)], b_sems)
    a_copies = copy_blocks(
        [(ref.at[pl.ds(0, A_ROWS)], a_ref.at[pl.ds(m * A_ROWS, A_ROWS)])
         for m, ref in enumerate(a_in)], a_sems)

    def rank(n, dist_ref, mine, at_ref, out):
        def body(r, count):
            out[r] = count
            at_ref[count] = r
            return count + jnp.where(dist_ref[r] == mine, 1, 0)
        lax.fori_loop(0, n, body, jnp.int32(0), unroll=8)

    rank(MR, rdist_ref, where_ref[0], row_at, row_place)
    rank(MC, cdist_ref, where_ref[1], col_at, col_place)

    def clear(n, _):
        slot_ref[n] = jnp.int32(0)
        return 0

    lax.fori_loop(0, RL * CL, clear, 0, unroll=8)

    def pattern(n, _):
        at = row_place[cidx_ref[n, 0]] * CL + col_place[cidx_ref[n, 1]]
        slot_ref[at] = n + 1
        place_ref[n] = at
        return 0

    lax.fori_loop(0, CT, pattern, 0, unroll=4)
    acc_ref[...] = jnp.zeros_like(acc_ref)
    out_ref[...] = jnp.zeros_like(out_ref)
    for copy in raw_copies:
        copy.wait()
    lane = lanes_of((8, TILE))
    sub = rows_of((8, TILE))
    b_labels = read_labels(b_raw)
    packed = jnp.zeros((8, TILE), jnp.float32)
    for m in range(n_b):
        packed += pltpu.roll(jnp.where(lane < BTD, b_labels[m] + 1, 0.0), 16 * m, 1)
    hot_k = (packed[0:1] - 1 == rows_of((KW, TILE)).astype(jnp.float32)).astype(jnp.float32)
    row_col = jnp.zeros((8, TILE), jnp.float32)
    for i in range(RL):
        row_col = jnp.where(sub == i, row_at[i].astype(jnp.float32), row_col)
    slot_b = jnp.zeros((8, TILE), jnp.float32)
    for j in range(CL):
        column = jnp.zeros((8, TILE), jnp.float32)
        for i in range(RL):
            column = jnp.where(sub == i, slot_ref[i * CL + j].astype(jnp.float32), column)
        slot_b = jnp.where(packed[1:2] - 1 == col_at[j].astype(jnp.float32), column, slot_b)

    total = make_list(n_a, read_labels(a_raw), row_col, hot_k, slot_b, list_v)
    store_list(list_v, list_ref, list_sem)
    for copy in b_copies + a_copies:
        copy.wait()
    add_products(total, list_ref, a_ref, b_ref, acc_ref)

    def finish(n, _):
        out_ref[place_ref[n]] = acc_ref[n].astype(jnp.bfloat16)
        return 0

    lax.fori_loop(0, CT, finish, 0, unroll=4)


def label_kernel(
    a_ref, a_index_ref, b_ref, b_index_ref, a_out, b_out,
    a_index_v, a_labels, a_sems, b_index_v, b_labels, b_sems,
):
    sides = (
        (a_ref, a_index_ref, a_out, a_index_v, a_labels, a_sems),
        (b_ref, b_index_ref, b_out, b_index_v, b_labels, b_sems),
    )
    waits = []
    for tiles_ref, index_ref, out_ref, index_v, labels_ref, sems in sides:
        n = tiles_ref.shape[0]
        index_copy = pltpu.make_async_copy(index_ref, index_v, sems.at[1])
        index_copy.start()
        tiles_copy = pltpu.make_async_copy(tiles_ref, out_ref.at[pl.ds(0, n)], sems.at[0])
        tiles_copy.start()
        labels_ref[...] = jnp.zeros_like(labels_ref)
        waits.append((tiles_copy, index_copy))
    for (tiles_copy, index_copy), side in zip(waits, sides):
        tiles_ref, _, out_ref, index_v, labels_ref, _ = side
        n = tiles_ref.shape[0]
        index_copy.wait()
        labels_ref[0:2, 0:n // TILE] = index_v[...].astype(jnp.float32)
        out_ref[n:n + LABEL] = labels_ref[...].astype(jnp.bfloat16)
    for tiles_copy, _ in waits:
        tiles_copy.wait()


def per_device(a_tiles, a_index, b_tiles, b_index, row_dist, col_dist, c_index):
    core = lax.axis_index("col") % 2
    where = jnp.stack([lax.axis_index("row"), lax.axis_index("col")]).astype(jnp.int32)
    tokens = []

    def by_core(first, second):
        return jnp.where(core == 0, first, second)

    def after(x, *others):
        tied = lax.optimization_barrier((x, *[other[:16] for other in others]))
        tokens.extend(tied[1:])
        return tied[0]

    a_own, b_own = with_labels(a_tiles, a_index, b_tiles, b_index)
    b_far = row_move(b_own, dz=1)
    b_first = b_own
    far = col_move(a_own, dz=1)
    up0, down0 = col_move(a_own, dy=1), col_move(a_own, dy=-1)
    b_up0, b_down0 = row_move(b_first, dx=1), row_move(b_first, dx=-1)
    pick0 = by_core(up0, down0)
    across0 = col_move(pick0, dy=1, by_core=True)
    b_pick0 = by_core(b_up0, b_down0)
    b_across0 = row_move_by_core(after(b_pick0, pick0))
    b_sent = b_far
    b_up1, b_down1 = row_move(b_sent, dx=1), row_move(b_sent, dx=-1)
    far_sent = after(far, pick0)
    up1, down1 = col_move(far_sent, dy=1), col_move(far_sent, dy=-1)
    b_across1 = row_move_by_core(by_core(b_up1, b_down1))
    across1 = col_move(across0, dz=1)
    a_blocks = [a_own, up0, down0, across0, far, up1, down1, across1]
    sent = [a_own, up0, down0, across0, far, up1, down1, across1]
    a_blocks += [col_move(block, dc=1) for block in sent]
    b_blocks = [b_own, b_up0, b_down0, b_across0, b_far, b_up1, b_down1, b_across1]
    vmem = pl.BlockSpec(memory_space=pltpu.VMEM)
    smem = pl.BlockSpec(memory_space=pltpu.SMEM)
    anywhere = pl.BlockSpec(memory_space=pl.ANY)
    i32 = jnp.int32
    n_a, n_b, n_t = len(a_blocks), len(b_blocks), len(tokens)

    placed = [
        x if n in LAST else pltpu.with_memory_space_constraint(x, pltpu.HBM)
        for n, x in enumerate(a_blocks + b_blocks)
    ]

    def kernel(*refs):
        inputs = 4 + n_a + n_b
        product_kernel(n_a, n_b, *refs[:inputs], *refs[inputs + n_t:])

    out = pl.pallas_call(
        kernel,
        out_shape=jax.ShapeDtypeStruct((RL * CL, TILE, TILE), jnp.bfloat16),
        in_specs=[smem] * 4 + [anywhere] * (n_a + n_b + n_t),
        out_specs=vmem,
        scratch_shapes=[
            pltpu.VMEM((CT + 1, TILE, TILE), jnp.float32),
            pltpu.VMEM((n_a * A_ROWS, TILE), jnp.bfloat16),
            pltpu.VMEM((n_b * B_ROWS, TILE), jnp.bfloat16),
            pltpu.VMEM((n_a, LABEL, TILE), jnp.bfloat16),
            pltpu.VMEM((n_b, LABEL, TILE), jnp.bfloat16),
            pltpu.VMEM((8, TILE), i32),
            pltpu.SMEM((MR,), i32),
            pltpu.SMEM((MC,), i32),
            pltpu.SMEM((MR,), i32),
            pltpu.SMEM((MC,), i32),
            pltpu.SMEM((RL * CL,), i32),
            pltpu.SMEM((CT,), i32),
            pltpu.SMEM((8, TILE), i32),
            pltpu.SemaphoreType.DMA((n_a,)),
            pltpu.SemaphoreType.DMA((n_b,)),
            pltpu.SemaphoreType.DMA((n_a + n_b,)),
            pltpu.SemaphoreType.DMA,
        ],
        compiler_params=pltpu.CompilerParams(vmem_limit_bytes=20 << 20),
        cost_estimate=pl.CostEstimate(flops=3_000_000_000, bytes_accessed=14_000_000, transcendentals=0),
    )(where, row_dist, col_dist, c_index, *placed, *tokens)
    return out.reshape(RL, CL, TILE, TILE)


def solution(mesh):
    in_specs = (
        P(("row", "col"), None, None),
        P(("row", "col"), None),
        P(("row", "col"), None, None),
        P(("row", "col"), None),
        P(),
        P(),
        P(("row", "col"), None),
    )
    out_specs = P("row", "col", None, None)
    return jax.shard_map(
        per_device, mesh=mesh, in_specs=in_specs, out_specs=out_specs, check_vma=False
    )
```

```python
import functools

import jax
import jax.numpy as jnp
from jax import lax
from jax.experimental import pallas as pl
from jax.experimental.pallas import tpu as pltpu
from jax.sharding import PartitionSpec as P

TILE = 128
RL = 8
CL = 6
KW = 64
MR = 64
MC = 96
ATD = 17
BTD = 10
CT = 24
N_ROW = 8
N_COL = 16
LABEL = 16
A_ROWS = ATD * TILE
B_ROWS = BTD * TILE
A_BLOCK = A_ROWS + LABEL
B_BLOCK = B_ROWS + LABEL
LIST = 640
LAST = (5, 6, 7, 13, 14, 15)
GROUP = 32


def col_move(x, dy=0, dz=0, dc=0, by_core=False):
    pairs = []
    for i in range(N_COL):
        y, z, c = i // 4, i // 2 % 2, i % 2
        step = -dy if by_core and c else dy
        pairs.append((i, (y + step) % 4 * 4 + (z + dz) % 2 * 2 + (c + dc) % 2))
    return lax.ppermute(x, "col", pairs)


def row_move(x, dx=0, dz=0):
    pairs = []
    for i in range(N_ROW):
        z, xx = i // 4, i % 4
        pairs.append((i, (z + dz) % 2 * 4 + (xx + dx) % 4))
    return lax.ppermute(x, "row", pairs)


def row_move_by_core(x):
    pairs = []
    for p in range(N_ROW):
        for q in range(N_COL):
            step = -1 if q % 2 else 1
            pairs.append((p * N_COL + q, (p // 4 * 4 + (p % 4 + step) % 4) * N_COL + q))
    return lax.ppermute(x, ("row", "col"), pairs)


def with_labels(a_tiles, a_index, b_tiles, b_index):
    inputs, shapes, scratch = [], [], []
    for tiles, index in ((a_tiles, a_index), (b_tiles, b_index)):
        n = tiles.shape[0] * TILE
        inputs += [tiles.reshape(n, TILE), index.T]
        shapes.append(jax.ShapeDtypeStruct((n + LABEL, TILE), jnp.bfloat16))
        scratch += [
            pltpu.VMEM((2, tiles.shape[0]), jnp.int32),
            pltpu.VMEM((LABEL, TILE), jnp.float32),
            pltpu.SemaphoreType.DMA((2,)),
        ]
    return pl.pallas_call(
        label_kernel,
        out_shape=tuple(shapes),
        in_specs=[pl.BlockSpec(memory_space=pl.ANY)] * 4,
        out_specs=(pl.BlockSpec(memory_space=pltpu.VMEM),) * 2,
        scratch_shapes=scratch,
        compiler_params=pltpu.CompilerParams(vmem_limit_bytes=3 << 20),
    )(*[pltpu.with_memory_space_constraint(x, pltpu.HBM) for x in inputs])


def copy_blocks(pieces, sems):
    copies = []
    for n, (src, dst) in enumerate(pieces):
        copy = pltpu.make_async_copy(src, dst, sems.at[n])
        copy.start()
        copies.append(copy)
    return copies


def read_labels(raw_ref):
    return raw_ref[:, :8, :].astype(jnp.float32)


def lanes_of(shape):
    return lax.broadcasted_iota(jnp.int32, shape, len(shape) - 1)


def rows_of(shape):
    return lax.broadcasted_iota(jnp.int32, shape, len(shape) - 2)


def small_dot(a, b, contract):
    return lax.dot_general(
        a.astype(jnp.bfloat16), b.astype(jnp.bfloat16), ((contract[:1], contract[1:]), ((), ())),
        preferred_element_type=jnp.float32,
    )


def make_list(n_blocks, labels, row_col, hot_k, slot_b, list_v):
    lane = lanes_of((8, TILE))
    sub = rows_of((8, TILE))
    one_up = jnp.where(lane < ATD, lane + 1, 0).astype(jnp.float32)
    k_rows = rows_of((KW, TILE)).astype(jnp.float32)
    held = jnp.zeros((16, KW), jnp.float32)
    for m in range(n_blocks):
        here = labels[m, 0:1, :] == row_col
        there = (labels[m, 1:2, :] == k_rows).astype(jnp.float32)
        tile = jnp.where(here, one_up, 0.0)
        block = jnp.where(here & (one_up > 0), float(m + 1), 0.0)
        held += small_dot(jnp.concatenate([tile, block]), there, (1, 1))
    found = small_dot(held, hot_k, (1, 0))
    tile, block = found[:8], found[8:]
    hit = (tile > 0) & (slot_b > 0)
    hits = hit.astype(jnp.float32)
    square = (TILE, TILE)
    before = (rows_of(square) < lanes_of(square)).astype(jnp.float32)
    place = small_dot(hits, before, (1, 0))
    in_row = small_dot(hits, jnp.ones(square, jnp.float32), (1, 0))
    for i in range(7):
        place += jnp.where(sub > i, in_row[i:i + 1], 0.0)
    place = jnp.where(hit, place, -1.0)
    total = jnp.sum(hits).astype(jnp.int32)
    b_tile = (lane - 6 * (lane >> 4)).astype(jnp.float32)
    fields = []
    for i in range(8):
        rows = (tile[i:i + 1] - 1, block[i:i + 1] - 1, b_tile[:1], CT + 1 - slot_b[i:i + 1])
        field = jnp.zeros((8, TILE), jnp.float32)
        for n, row in enumerate(rows):
            field = jnp.where(sub == n, row, field)
        fields.append(field)
    fields = jnp.concatenate(fields, axis=1).astype(jnp.bfloat16)

    for c in range(LIST // TILE):
        @pl.when(c * TILE < total)
        def _(c=c):
            spots = (rows_of(square) + c * TILE).astype(jnp.float32)
            chosen = jnp.concatenate(
                [(place[i:i + 1] == spots).astype(jnp.bfloat16) for i in range(8)], axis=1)
            got = small_dot(fields, chosen, (1, 1)).astype(jnp.int32)
            entry = got[0:1] + got[1:2] * ATD + got[2:3] * 512 + (CT - got[3:4]) * 65536
            list_v[c:c + 1, :] = entry
    return total


def store_list(list_v, list_ref, sem):
    copy = pltpu.make_async_copy(list_v, list_ref, sem)
    copy.start()
    copy.wait()


def add_products(total, list_ref, a_ref, b_ref, acc_ref):
    def body(g, _):
        found = []
        for u in range(GROUP):
            n = g * GROUP + u
            entry = list_ref[n >> 7, n & 127]
            a = pl.multiple_of((entry & 511) * TILE, TILE)
            b = pl.multiple_of(((entry >> 9) & 127) * TILE, TILE)
            product = jnp.dot(
                a_ref[pl.ds(a, TILE), :], b_ref[pl.ds(b, TILE), :],
                preferred_element_type=jnp.float32,
            )
            found.append((entry >> 16, product))
        for slot, product in found:
            acc_ref[slot] += product
        return 0

    lax.fori_loop(0, (total + GROUP - 1) // GROUP, body, 0)


def product_kernel(
    n_a, n_b, where_ref, rdist_ref, cdist_ref, cidx_ref, *refs,
):
    a_in, b_in = refs[:n_a], refs[n_a:n_a + n_b]
    (out_ref, acc_ref, a_ref, b_ref, a_raw, b_raw, list_v,
     row_at, col_at, row_place, col_place, slot_ref, place_ref, list_ref,
     a_sems, b_sems, raw_sems, list_sem) = refs[n_a + n_b:]
    raw_copies = copy_blocks(
        [(ref.at[pl.ds(A_ROWS, LABEL)], a_raw.at[m]) for m, ref in enumerate(a_in)]
        + [(ref.at[pl.ds(B_ROWS, LABEL)], b_raw.at[m]) for m, ref in enumerate(b_in)], raw_sems)
    b_copies = copy_blocks(
        [(ref.at[pl.ds(0, B_ROWS)], b_ref.at[pl.ds(m * B_ROWS, B_ROWS)])
         for m, ref in enumerate(b_in)], b_sems)
    a_copies = copy_blocks(
        [(ref.at[pl.ds(0, A_ROWS)], a_ref.at[pl.ds(m * A_ROWS, A_ROWS)])
         for m, ref in enumerate(a_in)], a_sems)

    def rank(n, dist_ref, mine, at_ref, out):
        def body(r, count):
            out[r] = count
            at_ref[count] = r
            return count + jnp.where(dist_ref[r] == mine, 1, 0)
        lax.fori_loop(0, n, body, jnp.int32(0), unroll=8)

    rank(MR, rdist_ref, where_ref[0], row_at, row_place)
    rank(MC, cdist_ref, where_ref[1], col_at, col_place)

    def clear(n, _):
        slot_ref[n] = jnp.int32(0)
        return 0

    lax.fori_loop(0, RL * CL, clear, 0, unroll=8)

    def pattern(n, _):
        at = row_place[cidx_ref[n, 0]] * CL + col_place[cidx_ref[n, 1]]
        slot_ref[at] = n + 1
        place_ref[n] = at
        return 0

    lax.fori_loop(0, CT, pattern, 0, unroll=4)
    acc_ref[...] = jnp.zeros_like(acc_ref)
    out_ref[...] = jnp.zeros_like(out_ref)
    for copy in raw_copies:
        copy.wait()
    lane = lanes_of((8, TILE))
    sub = rows_of((8, TILE))
    b_labels = read_labels(b_raw)
    packed = jnp.zeros((8, TILE), jnp.float32)
    for m in range(n_b):
        packed += pltpu.roll(jnp.where(lane < BTD, b_labels[m] + 1, 0.0), 16 * m, 1)
    hot_k = (packed[0:1] - 1 == rows_of((KW, TILE)).astype(jnp.float32)).astype(jnp.float32)
    row_col = jnp.zeros((8, TILE), jnp.float32)
    for i in range(RL):
        row_col = jnp.where(sub == i, row_at[i].astype(jnp.float32), row_col)
    slot_b = jnp.zeros((8, TILE), jnp.float32)
    for j in range(CL):
        column = jnp.zeros((8, TILE), jnp.float32)
        for i in range(RL):
            column = jnp.where(sub == i, slot_ref[i * CL + j].astype(jnp.float32), column)
        slot_b = jnp.where(packed[1:2] - 1 == col_at[j].astype(jnp.float32), column, slot_b)

    labels = read_labels(a_raw)
    half = n_a // 2
    for part in range(2):
        blocks = slice(part * half, (part + 1) * half)
        total = make_list(half, labels[blocks], row_col, hot_k, slot_b, list_v)
        store_list(list_v, list_ref, list_sem)
        for copy in (b_copies if part == 0 else []) + a_copies[blocks]:
            copy.wait()
        held = a_ref.at[pl.ds(part * half * A_ROWS, half * A_ROWS)]
        add_products(total, list_ref, held, b_ref, acc_ref)

    def finish(n, _):
        out_ref[place_ref[n]] = acc_ref[n].astype(jnp.bfloat16)
        return 0

    lax.fori_loop(0, CT, finish, 0, unroll=4)


def label_kernel(
    a_ref, a_index_ref, b_ref, b_index_ref, a_out, b_out,
    a_index_v, a_labels, a_sems, b_index_v, b_labels, b_sems,
):
    sides = (
        (a_ref, a_index_ref, a_out, a_index_v, a_labels, a_sems),
        (b_ref, b_index_ref, b_out, b_index_v, b_labels, b_sems),
    )
    waits = []
    for tiles_ref, index_ref, out_ref, index_v, labels_ref, sems in sides:
        n = tiles_ref.shape[0]
        index_copy = pltpu.make_async_copy(index_ref, index_v, sems.at[1])
        index_copy.start()
        tiles_copy = pltpu.make_async_copy(tiles_ref, out_ref.at[pl.ds(0, n)], sems.at[0])
        tiles_copy.start()
        labels_ref[...] = jnp.zeros_like(labels_ref)
        waits.append((tiles_copy, index_copy))
    for (tiles_copy, index_copy), side in zip(waits, sides):
        tiles_ref, _, out_ref, index_v, labels_ref, _ = side
        n = tiles_ref.shape[0]
        index_copy.wait()
        labels_ref[0:2, 0:n // TILE] = index_v[...].astype(jnp.float32)
        out_ref[n:n + LABEL] = labels_ref[...].astype(jnp.bfloat16)
    for tiles_copy, _ in waits:
        tiles_copy.wait()


def per_device(a_tiles, a_index, b_tiles, b_index, row_dist, col_dist, c_index):
    core = lax.axis_index("col") % 2
    where = jnp.stack([lax.axis_index("row"), lax.axis_index("col")]).astype(jnp.int32)
    tokens = []

    def by_core(first, second):
        return jnp.where(core == 0, first, second)

    def after(x, *others):
        tied = lax.optimization_barrier((x, *[other[:16] for other in others]))
        tokens.extend(tied[1:])
        return tied[0]

    a_own, b_own = with_labels(a_tiles, a_index, b_tiles, b_index)
    b_far = row_move(b_own, dz=1)
    b_first = b_own
    far = col_move(a_own, dz=1)
    up0, down0 = col_move(a_own, dy=1), col_move(a_own, dy=-1)
    b_up0, b_down0 = row_move(b_first, dx=1), row_move(b_first, dx=-1)
    pick0 = by_core(up0, down0)
    across0 = col_move(pick0, dy=1, by_core=True)
    b_pick0 = by_core(b_up0, b_down0)
    b_across0 = row_move_by_core(after(b_pick0, pick0))
    b_sent = b_far
    b_up1, b_down1 = row_move(b_sent, dx=1), row_move(b_sent, dx=-1)
    far_sent = after(far, pick0)
    up1, down1 = col_move(far_sent, dy=1), col_move(far_sent, dy=-1)
    b_across1 = row_move_by_core(by_core(b_up1, b_down1))
    across1 = col_move(across0, dz=1)
    a_blocks = [a_own, up0, down0, across0, far, up1, down1, across1]
    sent = [a_own, up0, down0, across0, far, up1, down1, across1]
    a_blocks += [col_move(block, dc=1) for block in sent]
    b_blocks = [b_own, b_up0, b_down0, b_across0, b_far, b_up1, b_down1, b_across1]
    vmem = pl.BlockSpec(memory_space=pltpu.VMEM)
    smem = pl.BlockSpec(memory_space=pltpu.SMEM)
    anywhere = pl.BlockSpec(memory_space=pl.ANY)
    i32 = jnp.int32
    n_a, n_b, n_t = len(a_blocks), len(b_blocks), len(tokens)

    placed = [
        x if n in LAST else pltpu.with_memory_space_constraint(x, pltpu.HBM)
        for n, x in enumerate(a_blocks + b_blocks)
    ]

    def kernel(*refs):
        inputs = 4 + n_a + n_b
        product_kernel(n_a, n_b, *refs[:inputs], *refs[inputs + n_t:])

    out = pl.pallas_call(
        kernel,
        out_shape=jax.ShapeDtypeStruct((RL * CL, TILE, TILE), jnp.bfloat16),
        in_specs=[smem] * 4 + [anywhere] * (n_a + n_b + n_t),
        out_specs=vmem,
        scratch_shapes=[
            pltpu.VMEM((CT + 1, TILE, TILE), jnp.float32),
            pltpu.VMEM((n_a * A_ROWS, TILE), jnp.bfloat16),
            pltpu.VMEM((n_b * B_ROWS, TILE), jnp.bfloat16),
            pltpu.VMEM((n_a, LABEL, TILE), jnp.bfloat16),
            pltpu.VMEM((n_b, LABEL, TILE), jnp.bfloat16),
            pltpu.VMEM((8, TILE), i32),
            pltpu.SMEM((MR,), i32),
            pltpu.SMEM((MC,), i32),
            pltpu.SMEM((MR,), i32),
            pltpu.SMEM((MC,), i32),
            pltpu.SMEM((RL * CL,), i32),
            pltpu.SMEM((CT,), i32),
            pltpu.SMEM((8, TILE), i32),
            pltpu.SemaphoreType.DMA((n_a,)),
            pltpu.SemaphoreType.DMA((n_b,)),
            pltpu.SemaphoreType.DMA((n_a + n_b,)),
            pltpu.SemaphoreType.DMA,
        ],
        compiler_params=pltpu.CompilerParams(vmem_limit_bytes=20 << 20),
        cost_estimate=pl.CostEstimate(flops=3_000_000_000, bytes_accessed=14_000_000, transcendentals=0),
    )(where, row_dist, col_dist, c_index, *placed, *tokens)
    return out.reshape(RL, CL, TILE, TILE)


def solution(mesh):
    in_specs = (
        P(("row", "col"), None, None),
        P(("row", "col"), None),
        P(("row", "col"), None, None),
        P(("row", "col"), None),
        P(),
        P(),
        P(("row", "col"), None),
    )
    out_specs = P("row", "col", None, None)
    return jax.shard_map(
        per_device, mesh=mesh, in_specs=in_specs, out_specs=out_specs, check_vma=False
    )
```

```python
import functools

import jax
import jax.numpy as jnp
from jax import lax
from jax.experimental import pallas as pl
from jax.experimental.pallas import tpu as pltpu
from jax.sharding import PartitionSpec as P

TILE = 128
RL = 8
CL = 6
KW = 64
MR = 64
MC = 96
ATD = 17
BTD = 10
CT = 24
N_ROW = 8
N_COL = 16
LABEL = 16
A_ROWS = ATD * TILE
B_ROWS = BTD * TILE
A_BLOCK = A_ROWS + LABEL
B_BLOCK = B_ROWS + LABEL
LIST = 640
LAST = (3, 5, 6, 7, 11, 13, 14, 15)
GROUP = 32


def col_move(x, dy=0, dz=0, dc=0, by_core=False):
    pairs = []
    for i in range(N_COL):
        y, z, c = i // 4, i // 2 % 2, i % 2
        step = -dy if by_core and c else dy
        pairs.append((i, (y + step) % 4 * 4 + (z + dz) % 2 * 2 + (c + dc) % 2))
    return lax.ppermute(x, "col", pairs)


def row_move(x, dx=0, dz=0):
    pairs = []
    for i in range(N_ROW):
        z, xx = i // 4, i % 4
        pairs.append((i, (z + dz) % 2 * 4 + (xx + dx) % 4))
    return lax.ppermute(x, "row", pairs)


def row_move_by_core(x):
    pairs = []
    for p in range(N_ROW):
        for q in range(N_COL):
            step = -1 if q % 2 else 1
            pairs.append((p * N_COL + q, (p // 4 * 4 + (p % 4 + step) % 4) * N_COL + q))
    return lax.ppermute(x, ("row", "col"), pairs)


def with_labels(a_tiles, a_index, b_tiles, b_index):
    inputs, shapes, scratch = [], [], []
    for tiles, index in ((a_tiles, a_index), (b_tiles, b_index)):
        n = tiles.shape[0] * TILE
        inputs += [tiles.reshape(n, TILE), index.T]
        shapes.append(jax.ShapeDtypeStruct((n + LABEL, TILE), jnp.bfloat16))
        scratch += [
            pltpu.VMEM((2, tiles.shape[0]), jnp.int32),
            pltpu.VMEM((LABEL, TILE), jnp.float32),
            pltpu.SemaphoreType.DMA((2,)),
        ]
    return pl.pallas_call(
        label_kernel,
        out_shape=tuple(shapes),
        in_specs=[pl.BlockSpec(memory_space=pl.ANY)] * 4,
        out_specs=(pl.BlockSpec(memory_space=pltpu.VMEM),) * 2,
        scratch_shapes=scratch,
        compiler_params=pltpu.CompilerParams(vmem_limit_bytes=3 << 20),
    )(*[pltpu.with_memory_space_constraint(x, pltpu.HBM) for x in inputs])


def copy_blocks(pieces, sems):
    copies = []
    for n, (src, dst) in enumerate(pieces):
        copy = pltpu.make_async_copy(src, dst, sems.at[n])
        copy.start()
        copies.append(copy)
    return copies


def read_labels(raw_ref):
    return raw_ref[:, :8, :].astype(jnp.float32)


def lanes_of(shape):
    return lax.broadcasted_iota(jnp.int32, shape, len(shape) - 1)


def rows_of(shape):
    return lax.broadcasted_iota(jnp.int32, shape, len(shape) - 2)


def small_dot(a, b, contract):
    return lax.dot_general(
        a.astype(jnp.bfloat16), b.astype(jnp.bfloat16), ((contract[:1], contract[1:]), ((), ())),
        preferred_element_type=jnp.float32,
    )


def make_list(n_blocks, labels, row_col, hot_k, slot_b, list_v):
    lane = lanes_of((8, TILE))
    sub = rows_of((8, TILE))
    one_up = jnp.where(lane < ATD, lane + 1, 0).astype(jnp.float32)
    k_rows = rows_of((KW, TILE)).astype(jnp.float32)
    held = jnp.zeros((16, KW), jnp.float32)
    for m in range(n_blocks):
        here = labels[m, 0:1, :] == row_col
        there = (labels[m, 1:2, :] == k_rows).astype(jnp.float32)
        tile = jnp.where(here, one_up, 0.0)
        block = jnp.where(here & (one_up > 0), float(m + 1), 0.0)
        held += small_dot(jnp.concatenate([tile, block]), there, (1, 1))
    found = small_dot(held, hot_k, (1, 0))
    tile, block = found[:8], found[8:]
    hit = (tile > 0) & (slot_b > 0)
    hits = hit.astype(jnp.float32)
    square = (TILE, TILE)
    before = (rows_of(square) < lanes_of(square)).astype(jnp.float32)
    place = small_dot(hits, before, (1, 0))
    in_row = small_dot(hits, jnp.ones(square, jnp.float32), (1, 0))
    for i in range(7):
        place += jnp.where(sub > i, in_row[i:i + 1], 0.0)
    place = jnp.where(hit, place, -1.0)
    total = jnp.sum(hits).astype(jnp.int32)
    b_tile = (lane - 6 * (lane >> 4)).astype(jnp.float32)
    fields = []
    for i in range(8):
        rows = (tile[i:i + 1] - 1, block[i:i + 1] - 1, b_tile[:1], CT + 1 - slot_b[i:i + 1])
        field = jnp.zeros((8, TILE), jnp.float32)
        for n, row in enumerate(rows):
            field = jnp.where(sub == n, row, field)
        fields.append(field)
    fields = jnp.concatenate(fields, axis=1).astype(jnp.bfloat16)

    for c in range(LIST // TILE):
        @pl.when(c * TILE < total)
        def _(c=c):
            spots = (rows_of(square) + c * TILE).astype(jnp.float32)
            chosen = jnp.concatenate(
                [(place[i:i + 1] == spots).astype(jnp.bfloat16) for i in range(8)], axis=1)
            got = small_dot(fields, chosen, (1, 1)).astype(jnp.int32)
            entry = got[0:1] + got[1:2] * ATD + got[2:3] * 512 + (CT - got[3:4]) * 65536
            list_v[c:c + 1, :] = entry
    return total


def store_list(list_v, list_ref, sem):
    copy = pltpu.make_async_copy(list_v, list_ref, sem)
    copy.start()
    copy.wait()


def add_products(total, list_ref, a_ref, b_ref, acc_ref):
    def body(g, _):
        found = []
        for u in range(GROUP):
            n = g * GROUP + u
            entry = list_ref[n >> 7, n & 127]
            a = pl.multiple_of((entry & 511) * TILE, TILE)
            b = pl.multiple_of(((entry >> 9) & 127) * TILE, TILE)
            product = jnp.dot(
                a_ref[pl.ds(a, TILE), :], b_ref[pl.ds(b, TILE), :],
                preferred_element_type=jnp.float32,
            )
            found.append((entry >> 16, product))
        for slot, product in found:
            acc_ref[slot] += product
        return 0

    lax.fori_loop(0, (total + GROUP - 1) // GROUP, body, 0)


def product_kernel(
    n_a, n_b, where_ref, rdist_ref, cdist_ref, cidx_ref, *refs,
):
    a_in, b_in = refs[:n_a], refs[n_a:n_a + n_b]
    (out_ref, acc_ref, a_ref, b_ref, a_raw, b_raw, list_v,
     row_at, col_at, row_place, col_place, slot_ref, place_ref, list_ref,
     a_sems, b_sems, raw_sems, list_sem) = refs[n_a + n_b:]
    raw_copies = copy_blocks(
        [(ref.at[pl.ds(A_ROWS, LABEL)], a_raw.at[m]) for m, ref in enumerate(a_in)]
        + [(ref.at[pl.ds(B_ROWS, LABEL)], b_raw.at[m]) for m, ref in enumerate(b_in)], raw_sems)
    b_copies = copy_blocks(
        [(ref.at[pl.ds(0, B_ROWS)], b_ref.at[pl.ds(m * B_ROWS, B_ROWS)])
         for m, ref in enumerate(b_in)], b_sems)
    a_copies = copy_blocks(
        [(ref.at[pl.ds(0, A_ROWS)], a_ref.at[pl.ds(m * A_ROWS, A_ROWS)])
         for m, ref in enumerate(a_in)], a_sems)

    def rank(n, dist_ref, mine, at_ref, out):
        def body(r, count):
            out[r] = count
            at_ref[count] = r
            return count + jnp.where(dist_ref[r] == mine, 1, 0)
        lax.fori_loop(0, n, body, jnp.int32(0), unroll=8)

    rank(MR, rdist_ref, where_ref[0], row_at, row_place)
    rank(MC, cdist_ref, where_ref[1], col_at, col_place)

    def clear(n, _):
        slot_ref[n] = jnp.int32(0)
        return 0

    lax.fori_loop(0, RL * CL, clear, 0, unroll=8)

    def pattern(n, _):
        at = row_place[cidx_ref[n, 0]] * CL + col_place[cidx_ref[n, 1]]
        slot_ref[at] = n + 1
        place_ref[n] = at
        return 0

    lax.fori_loop(0, CT, pattern, 0, unroll=4)
    acc_ref[...] = jnp.zeros_like(acc_ref)
    out_ref[...] = jnp.zeros_like(out_ref)
    for copy in raw_copies:
        copy.wait()
    lane = lanes_of((8, TILE))
    sub = rows_of((8, TILE))
    b_labels = read_labels(b_raw)
    packed = jnp.zeros((8, TILE), jnp.float32)
    for m in range(n_b):
        packed += pltpu.roll(jnp.where(lane < BTD, b_labels[m] + 1, 0.0), 16 * m, 1)
    hot_k = (packed[0:1] - 1 == rows_of((KW, TILE)).astype(jnp.float32)).astype(jnp.float32)
    row_col = jnp.zeros((8, TILE), jnp.float32)
    for i in range(RL):
        row_col = jnp.where(sub == i, row_at[i].astype(jnp.float32), row_col)
    slot_b = jnp.zeros((8, TILE), jnp.float32)
    for j in range(CL):
        column = jnp.zeros((8, TILE), jnp.float32)
        for i in range(RL):
            column = jnp.where(sub == i, slot_ref[i * CL + j].astype(jnp.float32), column)
        slot_b = jnp.where(packed[1:2] - 1 == col_at[j].astype(jnp.float32), column, slot_b)

    total = make_list(n_a, read_labels(a_raw), row_col, hot_k, slot_b, list_v)
    store_list(list_v, list_ref, list_sem)
    for copy in b_copies + a_copies:
        copy.wait()
    add_products(total, list_ref, a_ref, b_ref, acc_ref)

    def finish(n, _):
        out_ref[place_ref[n]] = acc_ref[n].astype(jnp.bfloat16)
        return 0

    lax.fori_loop(0, CT, finish, 0, unroll=4)


def label_kernel(
    a_ref, a_index_ref, b_ref, b_index_ref, a_out, b_out,
    a_index_v, a_labels, a_sems, b_index_v, b_labels, b_sems,
):
    sides = (
        (a_ref, a_index_ref, a_out, a_index_v, a_labels, a_sems),
        (b_ref, b_index_ref, b_out, b_index_v, b_labels, b_sems),
    )
    waits = []
    for tiles_ref, index_ref, out_ref, index_v, labels_ref, sems in sides:
        n = tiles_ref.shape[0]
        index_copy = pltpu.make_async_copy(index_ref, index_v, sems.at[1])
        index_copy.start()
        tiles_copy = pltpu.make_async_copy(tiles_ref, out_ref.at[pl.ds(0, n)], sems.at[0])
        tiles_copy.start()
        labels_ref[...] = jnp.zeros_like(labels_ref)
        waits.append((tiles_copy, index_copy))
    for (tiles_copy, index_copy), side in zip(waits, sides):
        tiles_ref, _, out_ref, index_v, labels_ref, _ = side
        n = tiles_ref.shape[0]
        index_copy.wait()
        labels_ref[0:2, 0:n // TILE] = index_v[...].astype(jnp.float32)
        out_ref[n:n + LABEL] = labels_ref[...].astype(jnp.bfloat16)
    for tiles_copy, _ in waits:
        tiles_copy.wait()


def per_device(a_tiles, a_index, b_tiles, b_index, row_dist, col_dist, c_index):
    core = lax.axis_index("col") % 2
    where = jnp.stack([lax.axis_index("row"), lax.axis_index("col")]).astype(jnp.int32)
    tokens = []

    def by_core(first, second):
        return jnp.where(core == 0, first, second)

    def after(x, *others):
        tied = lax.optimization_barrier((x, *[other[:16] for other in others]))
        tokens.extend(tied[1:])
        return tied[0]

    a_own, b_own = with_labels(a_tiles, a_index, b_tiles, b_index)
    b_far = row_move(b_own, dz=1)
    b_first = b_own
    far = col_move(a_own, dz=1)
    up0, down0 = col_move(a_own, dy=1), col_move(a_own, dy=-1)
    b_up0, b_down0 = row_move(b_first, dx=1), row_move(b_first, dx=-1)
    pick0 = by_core(up0, down0)
    across0 = col_move(pick0, dy=1, by_core=True)
    b_pick0 = by_core(b_up0, b_down0)
    b_across0 = row_move_by_core(after(b_pick0, pick0))
    b_sent = b_far
    b_up1, b_down1 = row_move(b_sent, dx=1), row_move(b_sent, dx=-1)
    far_sent = after(far, pick0)
    up1, down1 = col_move(far_sent, dy=1), col_move(far_sent, dy=-1)
    b_across1 = row_move_by_core(by_core(b_up1, b_down1))
    across1 = col_move(across0, dz=1)
    a_blocks = [a_own, up0, down0, across0, far, up1, down1, across1]
    sent = [a_own, up0, down0, across0, far, up1, down1, across1]
    a_blocks += [col_move(block, dc=1) for block in sent]
    b_blocks = [b_own, b_up0, b_down0, b_across0, b_far, b_up1, b_down1, b_across1]
    vmem = pl.BlockSpec(memory_space=pltpu.VMEM)
    smem = pl.BlockSpec(memory_space=pltpu.SMEM)
    anywhere = pl.BlockSpec(memory_space=pl.ANY)
    i32 = jnp.int32
    n_a, n_b, n_t = len(a_blocks), len(b_blocks), len(tokens)

    placed = [
        x if n in LAST else pltpu.with_memory_space_constraint(x, pltpu.HBM)
        for n, x in enumerate(a_blocks + b_blocks)
    ]

    def kernel(*refs):
        inputs = 4 + n_a + n_b
        product_kernel(n_a, n_b, *refs[:inputs], *refs[inputs + n_t:])

    out = pl.pallas_call(
        kernel,
        out_shape=jax.ShapeDtypeStruct((RL * CL, TILE, TILE), jnp.bfloat16),
        in_specs=[smem] * 4 + [anywhere] * (n_a + n_b + n_t),
        out_specs=vmem,
        scratch_shapes=[
            pltpu.VMEM((CT + 1, TILE, TILE), jnp.float32),
            pltpu.VMEM((n_a * A_ROWS, TILE), jnp.bfloat16),
            pltpu.VMEM((n_b * B_ROWS, TILE), jnp.bfloat16),
            pltpu.VMEM((n_a, LABEL, TILE), jnp.bfloat16),
            pltpu.VMEM((n_b, LABEL, TILE), jnp.bfloat16),
            pltpu.VMEM((8, TILE), i32),
            pltpu.SMEM((MR,), i32),
            pltpu.SMEM((MC,), i32),
            pltpu.SMEM((MR,), i32),
            pltpu.SMEM((MC,), i32),
            pltpu.SMEM((RL * CL,), i32),
            pltpu.SMEM((CT,), i32),
            pltpu.SMEM((8, TILE), i32),
            pltpu.SemaphoreType.DMA((n_a,)),
            pltpu.SemaphoreType.DMA((n_b,)),
            pltpu.SemaphoreType.DMA((n_a + n_b,)),
            pltpu.SemaphoreType.DMA,
        ],
        compiler_params=pltpu.CompilerParams(vmem_limit_bytes=20 << 20),
        cost_estimate=pl.CostEstimate(flops=3_000_000_000, bytes_accessed=14_000_000, transcendentals=0),
    )(where, row_dist, col_dist, c_index, *placed, *tokens)
    return out.reshape(RL, CL, TILE, TILE)


def solution(mesh):
    in_specs = (
        P(("row", "col"), None, None),
        P(("row", "col"), None),
        P(("row", "col"), None, None),
        P(("row", "col"), None),
        P(),
        P(),
        P(("row", "col"), None),
    )
    out_specs = P("row", "col", None, None)
    return jax.shard_map(
        per_device, mesh=mesh, in_specs=in_specs, out_specs=out_specs, check_vma=False
    )
```
